32 devices in a mesh: dp: 4 (over x, core), expert: 8 (over z, y).
Axes of the slice: x: 2, y: 2, z: 4, core: 2. Of those that a mesh axis runs over, the one named last changes fastest.
Arguments:
- tokens: bfloat16 [128, 2880], P(('dp', 'expert')), may hold values from -6 to 6
- cotangent: bfloat16 [128, 2880], P(('dp', 'expert')), may hold values from -6 to 6
- expert_ids: int32 [128, 4], P(('dp', 'expert')), may hold values from 0 to 7, all different within a row; in each aligned block of 4 rows (0 to 3, 4 to 7, ...) at most 2 rows name the same one
- route_weights: bfloat16 [128, 4], P(('dp', 'expert')), may hold values from 0.049804688 to 0.59765625
- gate_weight: bfloat16 [2880, 12288], P('dp', 'expert'), may hold values from -0.109375 to 0.109375
- up_weight: bfloat16 [2880, 12288], P('dp', 'expert'), may hold values from -0.109375 to 0.109375
- down_weight: bfloat16 [2880, 12288], P('dp', 'expert'), may hold values from -0.15625 to 0.15625
Outputs:
- d_tokens: bfloat16 [128, 2880], P(('dp', 'expert'))
- d_route: float32 [128, 4], P(('dp', 'expert'))
- grad_gate: bfloat16 [2880, 12288], P('dp', 'expert')
- grad_up: bfloat16 [2880, 12288], P('dp', 'expert')
- grad_down: bfloat16 [2880, 12288], P('dp', 'expert')
The draws below stay inside these ranges and needn't reach their ends.
Inputs may be any that keep to these rules, and one draw needn't show every extreme that they name: `expert_ids`: among the 4 tokens of one device, every expert is named by exactly 2 of them; a token names 4 different experts.
All inputs are finite; a program needn't handle non-finite values.
Results may differ from the reference program's by a relative error of at most 0.009.
Values may be sent and summed in bfloat16 or wider, within the bound.
No kernel may reach another device: no remote copies, remote signals or barrier semaphores. Data moves between devices by JAX's collectives and lax.ppermute only.
A program may use at most 192 MiB of HBM per device.

```python
import math
import jax
import jax.numpy as jnp
import numpy as np
from jax import lax

D = 2880
FF_WIN = 1536
EXPERTS_F = 8
TOPK = 4
TOK_DEV = 4
CAP = 2
TOKENS = 128
EF = 12288
N_DP = 4
N_EXPERT = 8


def block_levels(own_key, shape, split, least, largest):
    loudness, own = 1.0, jax.random.fold_in(own_key, 6)
    for dim, parts in split:
        heights = jnp.exp(jax.random.uniform(jax.random.fold_in(own, dim), (parts,), jnp.float32, least / len(split), largest / len(split)))
        loudness = loudness * jnp.repeat(heights, shape[dim] // parts).reshape([-1 if axis == dim else 1 for axis in range(len(shape))])
    return loudness


def assign_block(rng, own, number, rows, count, top, limit, skew):
    ranking = jax.random.permutation(rng, count)
    crowded, usual = portions_of(count, rows * top, limit, skew, True), portions_of(count, rows * top, limit, skew, False)
    places = jnp.arange(count)

    def named(sizes, rotation):
        used = int((sizes > 0).sum())
        fixed = max(1, used // 4)
        passed = fixed + (places - fixed + rotation * (used - fixed)) % max(1, count - fixed)
        return jnp.zeros((count,), jnp.int32).at[ranking[jnp.where(places < fixed, places, passed)]].set(jnp.asarray(sizes, jnp.int32))

    sizes = jnp.where(number % 4 == 0, named(crowded, number // 4), named(usual, number - number // 4 - 1))
    mixed = jax.random.permutation(jax.random.fold_in(own, 3), count)
    source_of, sink = mixed[0:count // 2 * 2:2], mixed[1:count // 2 * 2:2]
    margin = jnp.minimum(sizes[source_of] - 1, limit - sizes[sink]) // 2
    margin = jnp.where((source_of == ranking[0]) | (sink == ranking[0]) | (sizes[sink] == 0), 0, jnp.maximum(margin, 0))
    passed = jax.random.randint(jax.random.fold_in(own, 4), (count // 2,), 0, 1 << 20) % (margin + 1)
    sizes = sizes.at[source_of].add(-passed).at[sink].add(passed)
    items = jnp.searchsorted(jnp.cumsum(sizes), jnp.arange(rows * top), side="right").astype(jnp.int32)
    grid = items.reshape(top, rows).T
    grid = grid[jax.random.permutation(jax.random.fold_in(own, 1), rows)]
    rotation = jax.random.randint(jax.random.fold_in(own, 2), (rows, 1), 0, top)
    return jnp.take_along_axis(grid, (jnp.arange(top)[None, :] + rotation) % top, axis=1)


def portions_of(amount, total, reach, skew, full):
    portions = [(1 << 20) // math.isqrt(rank ** skew) + 1 for rank in range(1, amount + 1)]
    largest = reach if full else min(reach, max(-(-total // amount), total * portions[0] // sum(portions)))
    least = 1 if total - largest >= amount - 1 else 0
    counts, spare = [largest] + [least] * (amount - 1), total - largest - least * (amount - 1)
    while spare > 0:
        free = [i for i in range(1, amount) if counts[i] < largest] or [i for i in range(1, amount) if counts[i] < reach]
        pool, left = sum([portions[i] for i in free]), spare
        for i in free:
            more = min(reach - counts[i], max(1, left * portions[i] // pool), spare)
            counts[i] = counts[i] + more
            spare = spare - more
    return np.array(counts)


def centred(own_key, extent, width, bound, shards=(), held_as=jnp.bfloat16):
    result = jax.random.normal(own_key, extent, jnp.float32) * width
    if len(shards) > 0:
        result = block_levels(own_key, extent, shards, -0.22, 0.18) * result
    return jnp.clip(result, min=-bound, max=bound).astype(held_as)


def setup_inputs(seed: int = 0) -> dict:
    streams_of = jax.random.split(jax.random.key(seed), 8)
    tokens = centred(streams_of[0], (TOKENS, D), 1.0, 6.0, ((0, 32),))
    cotangent = centred(streams_of[1], (TOKENS, D), 1.0, 6.0, ((0, 32),))
    expert_ids_keys = jax.random.split(jax.random.fold_in(streams_of[2], 1), TOKENS // TOK_DEV)
    expert_ids_turns = jax.random.permutation(jax.random.fold_in(streams_of[2], 3), TOKENS // TOK_DEV)
    expert_ids = jax.vmap(lambda own, number: assign_block(jax.random.fold_in(streams_of[2], 2), own, number, TOK_DEV, EXPERTS_F, TOPK, CAP, 1))(expert_ids_keys, expert_ids_turns).reshape((TOKENS, TOPK))
    route_weights = jnp.clip(0.049804688 + 0.54785156 * jax.random.uniform(streams_of[3], (TOKENS, TOPK), jnp.float32) ** block_levels(streams_of[3], (TOKENS, TOPK), ((0, 32),), -0.2, 0.2), 0.049804688, 0.59765625).astype(jnp.bfloat16)
    gate_weight = centred(streams_of[4], (D, EF), D ** -0.5, 0.109375, ((0, 4), (1, 8)))
    up_weight = centred(streams_of[5], (D, EF), D ** -0.5, 0.109375, ((0, 4), (1, 8)))
    down_weight = centred(streams_of[6], (D, EF), FF_WIN ** -0.5, 0.15625, ((0, 4), (1, 8)))
    return {"tokens": tokens, "cotangent": cotangent, "expert_ids": expert_ids, "route_weights": route_weights, "gate_weight": gate_weight, "up_weight": up_weight, "down_weight": down_weight}


SLOPE = 1.702


def reference(tokens, cotangent, expert_ids, route_weights, gate_weight, up_weight, down_weight):
    count_all = tokens.shape[0]
    group_rows = count_all // N_DP
    shares = N_EXPERT // EXPERTS_F
    unit_dev = FF_WIN // shares
    d_total = jnp.zeros((count_all, D), jnp.float32)
    d_route = jnp.zeros((count_all, TOPK), jnp.float32)
    gate_parts = []
    up_parts = []
    down_parts = []
    tokens_grouped = tokens.astype(jnp.float32).reshape(N_DP, group_rows, D)
    for expert in range(EXPERTS_F):
        offset = expert * FF_WIN
        w_gate = lax.dynamic_slice_in_dim(gate_weight, offset, FF_WIN, 1)
        w_up = lax.dynamic_slice_in_dim(up_weight, offset, FF_WIN, 1)
        w_down = lax.dynamic_slice_in_dim(down_weight, offset, FF_WIN, 1)
        chosen = expert_ids == expert
        factor = jnp.sum(jnp.where(chosen, route_weights.astype(jnp.float32), 0.0), axis=1)[:, None]
        pre_gate = jnp.dot(tokens, w_gate, preferred_element_type=jnp.float32)
        pre_up = jnp.dot(tokens, w_up, preferred_element_type=jnp.float32)
        pulled = jnp.dot(cotangent, w_down, preferred_element_type=jnp.float32)
        sigma = jax.nn.sigmoid(SLOPE * pre_gate)
        active = pre_gate * sigma
        hidden = (pre_up + 1.0) * active
        d_gate = (factor * pulled * (pre_up + 1.0) * sigma * (1.0 + SLOPE * pre_gate * (1.0 - sigma))).astype(jnp.bfloat16)
        d_up = (factor * pulled * active).astype(jnp.bfloat16)
        products = hidden * pulled
        dots = jnp.zeros((count_all,), jnp.float32)
        for part in range(shares):
            lower = part * unit_dev
            piece = jnp.sum(products[:, lower:lower + unit_dev], axis=1).astype(jnp.bfloat16)
            dots = dots + lax.optimization_barrier(piece).astype(jnp.float32)
            term = jnp.dot(d_gate[:, lower:lower + unit_dev], w_gate[:, lower:lower + unit_dev].T, preferred_element_type=jnp.float32)
            term = term + jnp.dot(d_up[:, lower:lower + unit_dev], w_up[:, lower:lower + unit_dev].T, preferred_element_type=jnp.float32)
            term = term.astype(jnp.bfloat16)
            d_total = d_total + lax.optimization_barrier(term).astype(jnp.float32)
        d_route = d_route + jnp.where(chosen, dots[:, None], 0.0)
        hidden_low = hidden.astype(jnp.bfloat16)
        scaled = (factor * cotangent.astype(jnp.float32)).astype(jnp.bfloat16)
        gate_group = jnp.einsum("gri,grf->gif", tokens_grouped, d_gate.astype(jnp.float32).reshape(N_DP, group_rows, FF_WIN))
        up_group = jnp.einsum("gri,grf->gif", tokens_grouped, d_up.astype(jnp.float32).reshape(N_DP, group_rows, FF_WIN))
        down_group = jnp.einsum("gri,grf->gif", scaled.astype(jnp.float32).reshape(N_DP, group_rows, D), hidden_low.astype(jnp.float32).reshape(N_DP, group_rows, FF_WIN))
        gate_parts.append(jnp.sum(lax.optimization_barrier(gate_group.astype(jnp.bfloat16)).astype(jnp.float32), axis=0).astype(jnp.bfloat16))
        up_parts.append(jnp.sum(lax.optimization_barrier(up_group.astype(jnp.bfloat16)).astype(jnp.float32), axis=0).astype(jnp.bfloat16))
        down_parts.append(jnp.sum(lax.optimization_barrier(down_group.astype(jnp.bfloat16)).astype(jnp.float32), axis=0).astype(jnp.bfloat16))
    grad_gate = jnp.concatenate(gate_parts, axis=1)
    grad_up = jnp.concatenate(up_parts, axis=1)
    grad_down = jnp.concatenate(down_parts, axis=1)
    return d_total.astype(jnp.bfloat16), d_route, grad_gate, grad_up, grad_down
```

```python
import jax
import jax.numpy as jnp
from jax import lax
from jax.sharding import PartitionSpec as P

EXPERTS_F = 8
TOPK = 4
CORES = 2
LANES = 128


SLOPE = 1.702


def contract_rows(left, right):
    return lax.dot_general(
        left, right, (((0,), (0,)), ((), ())), preferred_element_type=jnp.float32
    )


def contract_cols(left, right):
    return lax.dot_general(
        left, right, (((1,), (1,)), ((), ())), preferred_element_type=jnp.float32
    )


def round_up(value, unit):
    return (value + unit - 1) // unit * unit


def local(tokens, cotangent, expert_ids, route_weights, gate_weight, up_weight, down_weight):
    n_dp = lax.axis_size("dp")
    members = lax.axis_size("expert")
    per_expert = members // EXPERTS_F
    sources = n_dp * members
    token_count, model_width = tokens.shape
    rows, hidden_units = gate_weight.shape
    half = hidden_units // CORES
    slots = token_count * TOPK // EXPERTS_F
    bf16 = jnp.bfloat16
    wide = round_up(rows // 2 + 1, LANES)

    expert_iota = lax.iota(jnp.int32, EXPERTS_F)
    hits = expert_ids[:, :, None] == expert_iota[None, None, :]
    picked = jnp.any(hits, axis=1)
    weight_each = jnp.sum(
        jnp.where(hits, route_weights[:, :, None].astype(jnp.float32), 0.0), axis=1
    )
    ranking = jnp.cumsum(picked.astype(jnp.int32), axis=0) - 1
    slot_iota = lax.iota(jnp.int32, slots)
    selector = picked.T[:, None, :] & (ranking.T[:, None, :] == slot_iota[None, :, None])
    select_float = selector.astype(jnp.float32)
    select_low = selector.astype(bf16)

    def bucket(x):
        b = jnp.einsum("ect,td->ecd", select_low, x, preferred_element_type=jnp.float32).astype(bf16)
        return b.reshape(EXPERTS_F, slots, n_dp, rows)

    bucket_tokens = bucket(tokens)
    bucket_grads = bucket(cotangent)
    bucket_factor = jnp.sum(select_float * weight_each.T[:, None, :], axis=2).astype(bf16)
    spare = 2 * wide - rows
    factor_pad = jnp.zeros((EXPERTS_F, slots, n_dp, spare), bf16).at[..., 0].set(bucket_factor[:, :, None])
    packed = jnp.stack(
        [jnp.concatenate([bucket_tokens, factor_pad], -1), jnp.concatenate([bucket_grads, factor_pad], -1)], axis=0
    ).reshape(2, EXPERTS_F, slots, n_dp, 2, wide)
    packed = packed.transpose(3, 1, 0, 4, 2, 5)
    packed = jnp.repeat(packed, per_expert, axis=1).reshape(sources, 4 * slots, wide)
    got = lax.all_to_all(packed, ("dp", "expert"), split_axis=0, concat_axis=0, tiled=True)
    got = got.reshape(sources, 2, 2, slots, wide).transpose(1, 0, 3, 2, 4).reshape(2, sources * slots, 2 * wide)
    inputs = got[0, :, :rows]
    upstream = got[1, :, :rows]
    factor = got[0, :, rows : rows + 1].astype(jnp.float32)
    count = sources * slots

    me = lax.axis_index("dp")
    core = lax.rem(me, CORES)
    part = jnp.stack(
        [
            jnp.dot(inputs, gate_weight, preferred_element_type=jnp.float32),
            jnp.dot(inputs, up_weight, preferred_element_type=jnp.float32),
            jnp.dot(upstream, down_weight, preferred_element_type=jnp.float32),
        ],
        axis=1,
    )
    keep = lax.dynamic_slice_in_dim(part, core * half, half, 2)
    send = lax.dynamic_slice_in_dim(part, (1 - core) * half, half, 2).astype(bf16)
    swap = [(i, i ^ 1) for i in range(n_dp)]
    pair = keep + lax.ppermute(send, "dp", swap).astype(jnp.float32)
    chips = n_dp // CORES
    pair_low = pair.astype(bf16)
    total = pair
    for shift in range(1, chips):
        perm = [(i, (i + shift * CORES) % n_dp) for i in range(n_dp)]
        total = total + lax.ppermute(pair_low, "dp", perm).astype(jnp.float32)
    pre_gate, pre_up, pulled = total[:, 0], total[:, 1], total[:, 2]
    sigma = jax.nn.sigmoid(SLOPE * pre_gate)
    active = pre_gate * sigma
    hidden = (pre_up + 1.0) * active
    dots = jnp.sum(hidden * pulled, axis=1, keepdims=True)
    d_gate = factor * pulled * (pre_up + 1.0) * sigma * (1.0 + SLOPE * pre_gate * (1.0 - sigma))
    d_up = factor * pulled * active
    own = jnp.stack([d_gate, d_up, hidden], axis=1).astype(bf16)
    other = lax.ppermute(own, "dp", swap)
    full = jnp.where(core == 0, jnp.concatenate([own, other], 2), jnp.concatenate([other, own], 2))
    d_gate, d_up, hidden_low = full[:, 0], full[:, 1], full[:, 2]

    d_inputs = contract_cols(d_gate, gate_weight) + contract_cols(d_up, up_weight)
    dots_high = dots.astype(bf16)
    dots_rest = (dots - dots_high.astype(jnp.float32)).astype(bf16)
    back_wide = round_up(rows + 2, LANES)
    back = jnp.concatenate(
        [d_inputs.astype(bf16), dots_high, dots_rest, jnp.zeros((count, back_wide - rows - 2), bf16)], axis=1
    ).reshape(sources, slots, back_wide)
    back = lax.all_to_all(back, ("dp", "expert"), split_axis=0, concat_axis=0, tiled=True)
    back = back.reshape(n_dp, members * slots, back_wide)

    scaled = (factor * upstream.astype(jnp.float32)).astype(bf16)
    grad_gate = contract_rows(inputs, d_gate).astype(bf16)
    grad_up = contract_rows(inputs, d_up).astype(bf16)
    grad_down = contract_rows(scaled, hidden_low).astype(bf16)

    select_dev = jnp.repeat(select_low, per_expert, axis=0).reshape(members * slots, token_count)
    d_tokens = jnp.einsum("st,nsd->tnd", select_dev, back[:, :, :rows], preferred_element_type=jnp.float32)
    d_tokens = d_tokens.astype(bf16).reshape(token_count, model_width)
    back_dots = back[:CORES, :, rows : rows + 2].astype(jnp.float32)
    expert_dots = jnp.sum(back_dots, axis=(0, 2)).reshape(EXPERTS_F, per_expert, slots).sum(axis=1)
    token_dots = jnp.sum(select_float * expert_dots[:, :, None], axis=1)
    d_route = jnp.sum(jnp.where(hits, token_dots.T[:, None, :], 0.0), axis=2)
    return (d_tokens, d_route, grad_gate, grad_up, grad_down)


def solution(mesh):
    in_specs = (
        P(("dp", "expert"), None),
        P(("dp", "expert"), None),
        P(("dp", "expert"), None),
        P(("dp", "expert"), None),
        P("dp", "expert"),
        P("dp", "expert"),
        P("dp", "expert"),
    )
    out_specs = (
        P(("dp", "expert"), None),
        P(("dp", "expert"), None),
        P("dp", "expert"),
        P("dp", "expert"),
        P("dp", "expert"),
    )
    return jax.shard_map(local, mesh=mesh, in_specs=in_specs, out_specs=out_specs, check_vma=False)
```

```python
import functools
import math

import jax
import jax.numpy as jnp
from jax import lax
from jax.experimental import pallas as pl
from jax.experimental.pallas import tpu as pltpu
from jax.sharding import PartitionSpec as P

EXPERTS_F = 8
TOPK = 4
CORES = 2
LANES = 128
PARTS = 4

SLOPE = 1.702
BF16 = jnp.bfloat16
F32 = jnp.float32
VMEM_LIMIT = 16 * 1024 * 1024


def round_up(value, unit):
    return (value + unit - 1) // unit * unit


def dot(left, right, contract):
    return lax.dot_general(left, right, (contract, ((), ())), preferred_element_type=F32)


def at_half(which, half, width, body):
    if width == half:
        body(0)
    elif half % LANES == 0:
        body(pl.multiple_of(which * half, LANES))
    else:
        for k in range(CORES):
            pl.when(which == k)(functools.partial(body, k * half))


def held_width(half):
    return half if half % LANES == 0 else CORES * half


def window(ref, which, half):
    if half % LANES:
        return ref
    return ref.at[:, pl.ds(pl.multiple_of(which * half, LANES), half)]


def my_core():
    return lax.rem(lax.axis_index("dp"), CORES)


def pack_kernel(*refs, n_dp, rows, wide, slots):
    far, out_ref, near, source, sems = refs[:4], refs[4], refs[5:9], refs[9], refs[10]
    copies = [pltpu.make_async_copy(far[i], near[i], sems.at[i]) for i in range(4)]
    for copy in copies:
        copy.start()
    ids_ref, weights_ref, tokens_ref, grads_ref = near
    count = tokens_ref.shape[0]
    lines = EXPERTS_F * PARTS * slots
    line = lax.broadcasted_iota(jnp.int32, (lines, 1), 0)
    expert = line // (PARTS * slots)
    part = (line // slots) % PARTS
    slot = line % slots
    column = lax.broadcasted_iota(jnp.int32, (lines, PARTS * count), 1)
    source[...] = jnp.zeros_like(source)
    for copy in copies:
        copy.wait()
    ids = ids_ref[...]
    route = weights_ref[...].astype(F32)
    seen = jnp.zeros((lines, 1), jnp.int32)
    factor = jnp.zeros((lines, 1), F32)
    spread = jnp.zeros((lines, PARTS * count), F32)
    for t in range(count):
        named = jnp.zeros((lines, 1), jnp.int32)
        value = jnp.zeros((lines, 1), F32)
        for k in range(TOPK):
            same = ids[t : t + 1, k : k + 1] == expert
            named = named + same.astype(jnp.int32)
            value = value + jnp.where(same, route[t : t + 1, k : k + 1], 0.0)
        chosen = (named > 0) & (seen == slot)
        seen = seen + (named > 0).astype(jnp.int32)
        factor = factor + jnp.where(chosen, value, 0.0)
        spread = spread + jnp.where(chosen & (column == part * count + t), 1.0, 0.0)
    spread = spread.astype(BF16)
    lane = lax.broadcasted_iota(jnp.int32, (lines, wide), 1)
    mark = (lane == rows - wide) & (part % 2 == 1)
    for j in range(n_dp):
        for which, ref in enumerate((tokens_ref, grads_ref)):
            first = 2 * which * count
            source[first : first + count, :] = ref[:, j * rows : j * rows + wide].astype(F32)
            source[first + count : first + 2 * count, 0 : rows - wide] = ref[
                :, j * rows + wide : (j + 1) * rows
            ].astype(F32)
        block = dot(spread, source[...].astype(BF16), ((1,), (0,)))
        out_ref[j * lines : (j + 1) * lines, :] = jnp.where(mark, factor, block).astype(BF16)


def stage_kernel(order_ref, gate_ref, up_ref, gate_out, up_out, sems, *, half):
    other = 1 - my_core()
    copies = [
        pltpu.make_async_copy(window(gate_ref, other, half), gate_out, sems.at[0]),
        pltpu.make_async_copy(window(up_ref, other, half), up_out, sems.at[1]),
    ]
    for copy in copies:
        copy.start()
    for copy in copies:
        copy.wait()


def project(which, half, i, left_ref, weight_ref, out_ref):
    def body(base):
        product = dot(left_ref[...], weight_ref[:, pl.ds(base, half)], ((1,), (0,)))
        out_ref[:, i * half : (i + 1) * half] = product.astype(out_ref.dtype)

    at_half(which, half, weight_ref.shape[1], body)


def send_kernel(
    got_ref, gate_other, up_other, gate_ref, down_ref,
    inputs_ref, upstream_ref, factor_ref, send_ref, gate_own, down_other, sems, *, rows, wide, slots, half,
):
    core = my_core()
    other = 1 - core
    down_copy = pltpu.make_async_copy(window(down_ref, other, half), down_other, sems.at[0])
    gate_copy = pltpu.make_async_copy(window(gate_ref, core, half), gate_own, sems.at[1])
    down_copy.start()
    gate_copy.start()
    per_block = PARTS * slots
    sources = got_ref.shape[0] // per_block
    group = math.gcd(sources, 32)
    lines = group * per_block
    lane = lax.broadcasted_iota(jnp.int32, (1, lines), 1)
    target = (lane % per_block) * group + lane // per_block
    move = (lax.broadcasted_iota(jnp.int32, (lines, lines), 0) == target).astype(F32).astype(BF16)
    for g in range(sources // group):
        block = dot(move, got_ref[g * lines : (g + 1) * lines, :], ((1,), (0,)))
        for s in range(slots):
            to = s * sources + g * group
            piece = [block[(p * slots + s) * group : (p * slots + s + 1) * group] for p in range(PARTS)]
            inputs_ref[to : to + group, 0:wide] = piece[0].astype(BF16)
            inputs_ref[to : to + group, wide:rows] = piece[1][:, : rows - wide].astype(BF16)
            upstream_ref[to : to + group, 0:wide] = piece[2].astype(BF16)
            upstream_ref[to : to + group, wide:rows] = piece[3][:, : rows - wide].astype(BF16)
            factor_ref[to : to + group, :] = piece[1][:, rows - wide : rows - wide + 1]
    project(other, half, 0, inputs_ref, gate_other, send_ref)
    project(other, half, 1, inputs_ref, up_other, send_ref)
    down_copy.wait()
    project(other, half, 2, upstream_ref, down_other, send_ref)
    gate_copy.wait()


def keep_kernel(inputs_ref, upstream_ref, gate_own, up_ref, down_ref, keep_ref, up_own, down_own, sems, *, half):
    core = my_core()
    up_copy = pltpu.make_async_copy(window(up_ref, core, half), up_own, sems.at[0])
    down_copy = pltpu.make_async_copy(window(down_ref, core, half), down_own, sems.at[1])
    up_copy.start()
    down_copy.start()
    project(core, half, 0, inputs_ref, gate_own, keep_ref)
    up_copy.wait()
    project(core, half, 1, inputs_ref, up_own, keep_ref)
    down_copy.wait()
    project(core, half, 2, upstream_ref, down_own, keep_ref)


def pair_kernel(keep_ref, got_ref, pair_ref, low_ref):
    pair = keep_ref[...] + got_ref[...].astype(F32)
    pair_ref[...] = pair
    low_ref[...] = pair.astype(BF16)


def derive_kernel(pair_ref, factor_ref, *refs, half):
    others, (own_ref, dots_ref) = refs[:-2], refs[-2:]
    factor = factor_ref[...]

    def total(i):
        columns = slice(i * half, (i + 1) * half)
        value = pair_ref[:, columns]
        for ref in others:
            value = value + ref[:, columns].astype(F32)
        return value

    pre_gate, pre_up, pulled = total(0), total(1), total(2)
    sigma = jax.nn.sigmoid(SLOPE * pre_gate)
    active = pre_gate * sigma
    hidden = (pre_up + 1.0) * active
    d_gate = factor * pulled * (pre_up + 1.0) * sigma * (1.0 + SLOPE * pre_gate * (1.0 - sigma))
    d_up = factor * pulled * active
    own_ref[:, 0:half] = d_gate.astype(BF16)
    own_ref[:, half : 2 * half] = d_up.astype(BF16)
    own_ref[:, 2 * half : 3 * half] = hidden.astype(BF16)
    dots_ref[...] = jnp.sum(hidden * pulled, axis=1, keepdims=True)


def back_product(core, half, derived_ref, gate_ref, up_ref, write):
    def body(base):
        value = dot(derived_ref[:, 0:half], gate_ref[:, pl.ds(base, half)], ((1,), (1,)))
        value = value + dot(derived_ref[:, half : 2 * half], up_ref[:, pl.ds(base, half)], ((1,), (1,)))
        write(value)

    at_half(core, half, gate_ref.shape[1], body)


def back_own_kernel(own_ref, gate_ref, up_ref, out_ref, *, half):
    def write(value):
        out_ref[...] = value

    back_product(my_core(), half, own_ref, gate_ref, up_ref, write)


def back_kernel(other_ref, own_part_ref, dots_ref, gate_ref, up_ref, out_ref, low, stacked, *, half, rows, back_wide, slots):
    per_block = PARTS * slots
    sources = out_ref.shape[0] // per_block
    group = math.gcd(sources, 32)
    lines = group * per_block

    def write(value):
        low[:, 0:rows] = (own_part_ref[...] + value).astype(BF16)

    if low.shape[1] > rows:
        low[:, rows:] = jnp.zeros((low.shape[0], low.shape[1] - rows), BF16)
    back_product(1 - my_core(), half, other_ref, gate_ref, up_ref, write)
    column = lax.broadcasted_iota(jnp.int32, (1, lines), 1)
    target = (column % group) * per_block + column // group
    move = (lax.broadcasted_iota(jnp.int32, (lines, lines), 0) == target).astype(F32).astype(BF16)
    dots = dots_ref[...]
    high = dots.astype(BF16).astype(F32)
    lane = lax.broadcasted_iota(jnp.int32, (dots.shape[0], back_wide), 1)
    last = jnp.where(lane == 0, high, jnp.where(lane == 1, dots - high, 0.0)).astype(BF16)
    for g in range(sources // group):
        for s in range(slots):
            here = s * sources + g * group
            for p in range(PARTS):
                to = (p * slots + s) * group
                if p == PARTS - 1:
                    stacked[to : to + group, :] = last[here : here + group]
                else:
                    stacked[to : to + group, :] = low[here : here + group, p * back_wide : (p + 1) * back_wide]
        out_ref[g * lines : (g + 1) * lines, :] = dot(move, stacked[...], ((1,), (0,))).astype(BF16)


def grad_kernel(inputs_ref, upstream_ref, factor_ref, own_ref, other_ref, gate_ref, up_ref, down_ref, *, half):
    core = my_core()
    scaled = (factor_ref[...] * upstream_ref[...].astype(F32)).astype(BF16)
    lefts = (inputs_ref[...], inputs_ref[...], scaled)
    for which, ref in ((core, own_ref), (1 - core, other_ref)):
        def body(base, ref=ref):
            for i, (left, out) in enumerate(zip(lefts, (gate_ref, up_ref, down_ref))):
                product = dot(left, ref[:, i * half : (i + 1) * half], ((0,), (0,)))
                out[:, pl.ds(base, half)] = product.astype(BF16)

        at_half(which, half, gate_ref.shape[1], body)


def combine_kernel(ids_ref, back_ref, tokens_ref, route_ref, gather, *, n_dp, rows, back_wide, slots, per_expert):
    count = tokens_ref.shape[0]
    lines = back_ref.shape[0] // n_dp
    line = lax.broadcasted_iota(jnp.int32, (1, lines), 1)
    expert = line // (PARTS * slots * per_expert)
    part = (line // slots) % PARTS
    slot = line % slots
    ids = ids_ref[...]
    seen = jnp.zeros((1, lines), jnp.int32)
    for t in range(count):
        same = [ids[t : t + 1, k : k + 1] == expert for k in range(TOPK)]
        named = functools.reduce(lambda a, b: a | b, same)
        chosen = named & (seen == slot)
        seen = seen + named.astype(jnp.int32)
        for p in range(PARTS - 1):
            gather[p * count + t : p * count + t + 1, :] = (chosen & (part == p)).astype(F32)
        for k in range(TOPK):
            row = (PARTS - 1 + k) * count + t
            gather[row : row + 1, :] = (chosen & same[k] & (part == PARTS - 1)).astype(F32)
    sums = gather[...].astype(BF16)
    route = jnp.zeros((TOPK * count, 1), F32)
    for j in range(n_dp):
        block = dot(sums, back_ref[j * lines : (j + 1) * lines, :], ((1,), (0,)))
        for p in range(PARTS - 1):
            width = min(back_wide, rows - p * back_wide)
            if width > 0:
                first = j * rows + p * back_wide
                tokens_ref[:, first : first + width] = block[p * count : (p + 1) * count, :width].astype(BF16)
        if j < CORES:
            terms = block[(PARTS - 1) * count : (PARTS - 1 + TOPK) * count]
            route = route + terms[:, 0:1] + terms[:, 1:2]
    for k in range(TOPK):
        route_ref[:, k : k + 1] = route[k * count : (k + 1) * count]


def call(kernel, outs, *args, scratch=(), flops=0, moved=0, far=(), limit=VMEM_LIMIT):
    args = [pltpu.with_memory_space_constraint(a, pltpu.HBM) if i in far else a for i, a in enumerate(args)]
    return pl.pallas_call(
        kernel,
        out_shape=outs,
        in_specs=[pl.BlockSpec(memory_space=pltpu.HBM if i in far else pltpu.VMEM) for i in range(len(args))],
        out_specs=jax.tree.map(lambda _: pl.BlockSpec(memory_space=pltpu.VMEM), outs),
        scratch_shapes=list(scratch),
        compiler_params=pltpu.CompilerParams(vmem_limit_bytes=limit),
        cost_estimate=pl.CostEstimate(flops=flops, bytes_accessed=moved, transcendentals=0),
    )(*args)


def shape(dims, dtype):
    return jax.ShapeDtypeStruct(dims, dtype)


def local(tokens, cotangent, expert_ids, route_weights, gate_weight, up_weight, down_weight):
    n_dp = lax.axis_size("dp")
    members = lax.axis_size("expert")
    per_expert = members // EXPERTS_F
    sources = n_dp * members
    token_count, model_width = tokens.shape
    rows, hidden_units = gate_weight.shape
    half = hidden_units // CORES
    slots = token_count * TOPK // EXPERTS_F
    count = sources * slots
    per_block = PARTS * slots
    wide = round_up(rows // 2 + 1, LANES)
    back_wide = round_up(-(-rows // (PARTS - 1)), LANES)
    group = math.gcd(sources, 32)

    packed = call(
        functools.partial(pack_kernel, n_dp=n_dp, rows=rows, wide=wide, slots=slots),
        shape((n_dp * EXPERTS_F * per_block, wide), BF16),
        expert_ids,
        route_weights,
        tokens,
        cotangent,
        scratch=[
            pltpu.VMEM(expert_ids.shape, jnp.int32),
            pltpu.VMEM(route_weights.shape, BF16),
            pltpu.VMEM(tokens.shape, BF16),
            pltpu.VMEM(cotangent.shape, BF16),
            pltpu.VMEM((PARTS * token_count, wide), F32),
            pltpu.SemaphoreType.DMA((4,)),
        ],
        moved=1 << 18,
        far=(0, 1, 2, 3),
    )
    packed = packed.reshape(n_dp, EXPERTS_F, per_block, wide)
    if per_expert > 1:
        packed = jnp.repeat(packed, per_expert, axis=1)
    packed = packed.reshape(sources, per_block, wide)
    got = lax.all_to_all(packed, ("dp", "expert"), split_axis=0, concat_axis=0, tiled=True)

    held = pltpu.VMEM((rows, held_width(half)), BF16)
    gate_other, up_other = call(
        functools.partial(stage_kernel, half=half),
        [held, held],
        packed,
        gate_weight,
        up_weight,
        scratch=[pltpu.SemaphoreType.DMA((2,))],
        moved=4 * rows * half,
        far=(0, 1, 2),
        limit=1 << 20,
    )

    inputs, upstream, factor, send, gate_own = call(
        functools.partial(send_kernel, rows=rows, wide=wide, slots=slots, half=half),
        [
            shape((count, rows), BF16),
            shape((count, rows), BF16),
            shape((count, 1), F32),
            shape((count, 3 * half), BF16),
            held,
        ],
        got.reshape(sources * per_block, wide),
        gate_other,
        up_other,
        gate_weight,
        down_weight,
        scratch=[held, pltpu.SemaphoreType.DMA((2,))],
        flops=6 * count * rows * half,
        moved=1 << 20,
        far=(3, 4),
    )
    swap = [(i, i ^ 1) for i in range(n_dp)]
    arrived = lax.ppermute(send, "dp", swap)
    keep, up_own = call(
        functools.partial(keep_kernel, half=half),
        [shape((count, 3 * half), F32), held],
        inputs,
        upstream,
        gate_own,
        up_weight,
        down_weight,
        scratch=[held, pltpu.SemaphoreType.DMA((2,))],
        flops=6 * count * rows * half,
        moved=1 << 20,
        far=(3, 4),
    )
    pair, low = call(
        pair_kernel,
        [shape((count, 3 * half), F32), shape((count, 3 * half), BF16)],
        keep,
        arrived,
        moved=1 << 20,
    )
    others = []
    for shift in range(1, n_dp // CORES):
        perm = [(i, (i + shift * CORES) % n_dp) for i in range(n_dp)]
        others.append(lax.ppermute(low, "dp", perm))
    own, dots = call(
        functools.partial(derive_kernel, half=half),
        [shape((count, 3 * half), BF16), shape((count, 1), F32)],
        pair,
        factor,
        *others,
        moved=1 << 20,
    )
    other = lax.ppermute(own, "dp", swap)
    own_part = call(
        functools.partial(back_own_kernel, half=half),
        shape((count, rows), F32),
        own,
        gate_own,
        up_own,
        flops=4 * count * rows * half,
        moved=1 << 20,
    )
    back = call(
        functools.partial(back_kernel, half=half, rows=rows, back_wide=back_wide, slots=slots),
        shape((sources * per_block, back_wide), BF16),
        other,
        own_part,
        dots,
        gate_other,
        up_other,
        scratch=[pltpu.VMEM((count, (PARTS - 1) * back_wide), BF16), pltpu.VMEM((group * per_block, back_wide), BF16)],
        flops=4 * count * rows * half,
        moved=1 << 20,
    )
    back = lax.all_to_all(
        back.reshape(sources, per_block, back_wide), ("dp", "expert"), split_axis=0, concat_axis=0, tiled=True
    )
    grads = call(
        functools.partial(grad_kernel, half=half),
        [shape((rows, hidden_units), BF16)] * 3,
        inputs,
        upstream,
        factor,
        own,
        other,
        flops=12 * count * rows * half,
        moved=6 * rows * hidden_units,
    )
    d_tokens, d_route = call(
        functools.partial(
            combine_kernel, n_dp=n_dp, rows=rows, back_wide=back_wide, slots=slots, per_expert=per_expert
        ),
        [shape((token_count, model_width), BF16), shape((token_count, TOPK), F32)],
        expert_ids,
        back.reshape(sources * per_block, back_wide),
        scratch=[pltpu.VMEM(((PARTS - 1 + TOPK) * token_count, members * per_block), F32)],
        moved=1 << 18,
    )
    return (d_tokens, d_route, *grads)


def solution(mesh):
    in_specs = (
        P(("dp", "expert"), None),
        P(("dp", "expert"), None),
        P(("dp", "expert"), None),
        P(("dp", "expert"), None),
        P("dp", "expert"),
        P("dp", "expert"),
        P("dp", "expert"),
    )
    out_specs = (
        P(("dp", "expert"), None),
        P(("dp", "expert"), None),
        P("dp", "expert"),
        P("dp", "expert"),
        P("dp", "expert"),
    )
    return jax.shard_map(local, mesh=mesh, in_specs=in_specs, out_specs=out_specs, check_vma=False)
```

```python
import functools
import math

import jax
import jax.numpy as jnp
from jax import lax
from jax.experimental import pallas as pl
from jax.experimental.pallas import tpu as pltpu
from jax.sharding import PartitionSpec as P

EXPERTS_F = 8
TOPK = 4
CORES = 2
LANES = 128
PARTS = 4

SLOPE = 1.702
BF16 = jnp.bfloat16
F32 = jnp.float32
VMEM_LIMIT = 16 * 1024 * 1024


def round_up(value, unit):
    return (value + unit - 1) // unit * unit


def dot(left, right, contract):
    return lax.dot_general(left, right, (contract, ((), ())), preferred_element_type=F32)


def at_half(which, half, width, body):
    if width == half:
        body(0)
    elif half % LANES == 0:
        body(pl.multiple_of(which * half, LANES))
    else:
        for k in range(CORES):
            pl.when(which == k)(functools.partial(body, k * half))


def chunks_of(half):
    return 2 if half % (2 * LANES) == 0 else 1


def window(ref, which, half, first, width):
    if half % LANES:
        return ref
    return ref.at[:, pl.ds(pl.multiple_of(which * half + first, LANES), width)]


def my_core():
    return lax.rem(lax.axis_index("dp"), CORES)


def pack_kernel(*refs, n_dp, rows, wide, slots):
    far, out_ref, near, source, sems = refs[:4], refs[4], refs[5:9], refs[9], refs[10]
    copies = [pltpu.make_async_copy(far[i], near[i], sems.at[i]) for i in range(4)]
    for copy in copies:
        copy.start()
    ids_ref, weights_ref, tokens_ref, grads_ref = near
    count = tokens_ref.shape[0]
    lines = EXPERTS_F * PARTS * slots
    line = lax.broadcasted_iota(jnp.int32, (lines, 1), 0)
    expert = line // (PARTS * slots)
    part = (line // slots) % PARTS
    slot = line % slots
    column = lax.broadcasted_iota(jnp.int32, (lines, PARTS * count), 1)
    source[...] = jnp.zeros_like(source)
    for copy in copies:
        copy.wait()
    ids = ids_ref[...]
    route = weights_ref[...].astype(F32)
    seen = jnp.zeros((lines, 1), jnp.int32)
    factor = jnp.zeros((lines, 1), F32)
    spread = jnp.zeros((lines, PARTS * count), F32)
    for t in range(count):
        named = jnp.zeros((lines, 1), jnp.int32)
        value = jnp.zeros((lines, 1), F32)
        for k in range(TOPK):
            same = ids[t : t + 1, k : k + 1] == expert
            named = named + same.astype(jnp.int32)
            value = value + jnp.where(same, route[t : t + 1, k : k + 1], 0.0)
        chosen = (named > 0) & (seen == slot)
        seen = seen + (named > 0).astype(jnp.int32)
        factor = factor + jnp.where(chosen, value, 0.0)
        spread = spread + jnp.where(chosen & (column == part * count + t), 1.0, 0.0)
    spread = spread.astype(BF16)
    lane = lax.broadcasted_iota(jnp.int32, (lines, wide), 1)
    mark = (lane == rows - wide) & (part % 2 == 1)
    for j in range(n_dp):
        for which, ref in enumerate((tokens_ref, grads_ref)):
            first = 2 * which * count
            source[first : first + count, :] = ref[:, j * rows : j * rows + wide].astype(F32)
            source[first + count : first + 2 * count, 0 : rows - wide] = ref[
                :, j * rows + wide : (j + 1) * rows
            ].astype(F32)
        block = dot(spread, source[...].astype(BF16), ((1,), (0,)))
        out_ref[j * lines : (j + 1) * lines, :] = jnp.where(mark, factor, block).astype(BF16)


def stage_kernel(order_ref, *refs, half):
    fars, nears, sems = refs[:3], refs[3:6], refs[6]
    other = 1 - my_core()
    copies = [
        pltpu.make_async_copy(window(far, other, half, 0, half), near, sems.at[i])
        for i, (far, near) in enumerate(zip(fars, nears))
    ]
    for copy in copies:
        copy.start()
    for copy in copies:
        copy.wait()


def project(base, width, i, left_ref, weight_ref, out_ref):
    product = dot(left_ref[...], weight_ref[:, pl.ds(base, width)], ((1,), (0,)))
    out_ref[:, i * width : (i + 1) * width] = product.astype(out_ref.dtype)


def send_kernel(
    got_ref, gate_ref, up_ref, down_ref, inputs_ref, upstream_ref, factor_ref, *send_refs, rows, wide, slots, half
):
    per_block = PARTS * slots
    sources = got_ref.shape[0] // per_block
    group = math.gcd(sources, 32)
    lines = group * per_block
    lane = lax.broadcasted_iota(jnp.int32, (1, lines), 1)
    target = (lane % per_block) * group + lane // per_block
    move = (lax.broadcasted_iota(jnp.int32, (lines, lines), 0) == target).astype(F32).astype(BF16)
    for g in range(sources // group):
        block = dot(move, got_ref[g * lines : (g + 1) * lines, :], ((1,), (0,)))
        for s in range(slots):
            to = s * sources + g * group
            piece = [block[(p * slots + s) * group : (p * slots + s + 1) * group] for p in range(PARTS)]
            inputs_ref[to : to + group, 0:wide] = piece[0].astype(BF16)
            inputs_ref[to : to + group, wide:rows] = piece[1][:, : rows - wide].astype(BF16)
            upstream_ref[to : to + group, 0:wide] = piece[2].astype(BF16)
            upstream_ref[to : to + group, wide:rows] = piece[3][:, : rows - wide].astype(BF16)
            factor_ref[to : to + group, :] = piece[1][:, rows - wide : rows - wide + 1]
    width = half // len(send_refs)

    def body(base):
        for q, send_ref in enumerate(send_refs):
            here = base + q * width
            project(here, width, 0, inputs_ref, gate_ref, send_ref)
            project(here, width, 1, inputs_ref, up_ref, send_ref)
            project(here, width, 2, upstream_ref, down_ref, send_ref)

    at_half(1 - my_core(), half, gate_ref.shape[1], body)


def keep_kernel(inputs_ref, upstream_ref, *refs, half, width, q):
    fars, keep_ref, nears, sems = refs[:3], refs[3], refs[4:7], refs[7]
    core = my_core()
    copies = [
        pltpu.make_async_copy(window(far, core, half, q * width, width), near, sems.at[i])
        for i, (far, near) in enumerate(zip(fars, nears))
    ]
    for copy in copies:
        copy.start()
    for i, (left_ref, near) in enumerate(zip((inputs_ref, inputs_ref, upstream_ref), nears)):
        copies[i].wait()
        at_half(
            core,
            width,
            near.shape[1],
            lambda base, i=i, left_ref=left_ref, near=near: project(base, width, i, left_ref, near, keep_ref),
        )


def pair_kernel(keep_ref, got_ref, pair_ref, low_ref):
    pair = keep_ref[...] + got_ref[...].astype(F32)
    pair_ref[...] = pair
    low_ref[...] = pair.astype(BF16)


def derive_kernel(pair_ref, factor_ref, *refs, half):
    others, (own_ref, dots_ref) = refs[:-2], refs[-2:]
    factor = factor_ref[...]

    def total(i):
        columns = slice(i * half, (i + 1) * half)
        value = pair_ref[:, columns]
        for ref in others:
            value = value + ref[:, columns].astype(F32)
        return value

    pre_gate, pre_up, pulled = total(0), total(1), total(2)
    sigma = jax.nn.sigmoid(SLOPE * pre_gate)
    active = pre_gate * sigma
    hidden = (pre_up + 1.0) * active
    d_gate = factor * pulled * (pre_up + 1.0) * sigma * (1.0 + SLOPE * pre_gate * (1.0 - sigma))
    d_up = factor * pulled * active
    own_ref[:, 0:half] = d_gate.astype(BF16)
    own_ref[:, half : 2 * half] = d_up.astype(BF16)
    own_ref[:, 2 * half : 3 * half] = hidden.astype(BF16)
    dots_ref[...] = jnp.sum(hidden * pulled, axis=1, keepdims=True)


def back_product(which, half, width, first, derived_ref, gate_ref, up_ref, write):
    def body(base):
        columns = pl.ds(base + first, width)
        value = dot(derived_ref[:, 0:width], gate_ref[:, columns], ((1,), (1,)))
        value = value + dot(derived_ref[:, width : 2 * width], up_ref[:, columns], ((1,), (1,)))
        write(value)

    at_half(which, half, gate_ref.shape[1], body)


def derive_back_kernel(pair_ref, factor_ref, gate_ref, up_ref, *refs, half):
    others, (own_ref, dots_ref, part_ref) = refs[:-3], refs[-3:]
    derive_kernel(pair_ref, factor_ref, *others, own_ref, dots_ref, half=half)

    def write(value):
        part_ref[...] = value

    back_product(my_core(), half, half, 0, own_ref, gate_ref, up_ref, write)


def back_part_kernel(own_ref, gate_own, up_own, *refs, half, width):
    out_ref = refs[-1]

    def write(value):
        out_ref[...] = value

    def add(value):
        out_ref[...] = out_ref[...] + value

    back_product(my_core(), width, width, 0, own_ref, gate_own, up_own, write)
    if len(refs) > 1:
        gate_other, up_other = refs[:2]
        earlier = refs[2:-1]
        for q in range(len(earlier) // 2):
            out_ref[...] = out_ref[...] + earlier[2 * q][...]
            back_product(1 - my_core(), half, width, q * width, earlier[2 * q + 1], gate_other, up_other, add)


def back_kernel(other_ref, part_ref, gate_ref, up_ref, *refs, half, width, first, rows, back_wide, slots):
    dots_refs, (out_ref, low, stacked) = refs[:-3], refs[-3:]
    per_block = PARTS * slots
    sources = out_ref.shape[0] // per_block
    group = math.gcd(sources, 32)
    lines = group * per_block

    def write(value):
        low[:, 0:rows] = (part_ref[...] + value).astype(BF16)

    if low.shape[1] > rows:
        low[:, rows:] = jnp.zeros((low.shape[0], low.shape[1] - rows), BF16)
    back_product(1 - my_core(), half, width, first, other_ref, gate_ref, up_ref, write)
    column = lax.broadcasted_iota(jnp.int32, (1, lines), 1)
    target = (column % group) * per_block + column // group
    move = (lax.broadcasted_iota(jnp.int32, (lines, lines), 0) == target).astype(F32).astype(BF16)
    dots = functools.reduce(lambda x, y: x + y, [ref[...] for ref in dots_refs])
    high = dots.astype(BF16).astype(F32)
    lane = lax.broadcasted_iota(jnp.int32, (dots.shape[0], back_wide), 1)
    last = jnp.where(lane == 0, high, jnp.where(lane == 1, dots - high, 0.0)).astype(BF16)
    for g in range(sources // group):
        for s in range(slots):
            here = s * sources + g * group
            for p in range(PARTS):
                to = (p * slots + s) * group
                if p == PARTS - 1:
                    stacked[to : to + group, :] = last[here : here + group]
                else:
                    stacked[to : to + group, :] = low[here : here + group, p * back_wide : (p + 1) * back_wide]
        out_ref[g * lines : (g + 1) * lines, :] = dot(move, stacked[...], ((1,), (0,))).astype(BF16)


def grad_kernel(inputs_ref, upstream_ref, factor_ref, *refs, half, width):
    derived, outs = refs[:-3], refs[-3:]
    core = my_core()
    scaled = (factor_ref[...] * upstream_ref[...].astype(F32)).astype(BF16)
    lefts = (inputs_ref[...], inputs_ref[...], scaled)
    for n, ref in enumerate(derived):

        def body(base, n=n, ref=ref):
            columns = pl.ds(base + (n // CORES) * width, width)
            for i, (left, out) in enumerate(zip(lefts, outs)):
                product = dot(left, ref[:, i * width : (i + 1) * width], ((0,), (0,)))
                out[:, columns] = product.astype(BF16)

        at_half(core if n % CORES == 0 else 1 - core, half, outs[0].shape[1], body)


def combine_kernel(ids_ref, back_ref, tokens_ref, route_ref, gather, *, n_dp, rows, back_wide, slots, per_expert):
    count = tokens_ref.shape[0]
    lines = back_ref.shape[0] // n_dp
    line = lax.broadcasted_iota(jnp.int32, (1, lines), 1)
    expert = line // (PARTS * slots * per_expert)
    part = (line // slots) % PARTS
    slot = line % slots
    ids = ids_ref[...]
    seen = jnp.zeros((1, lines), jnp.int32)
    for t in range(count):
        same = [ids[t : t + 1, k : k + 1] == expert for k in range(TOPK)]
        named = functools.reduce(lambda a, b: a | b, same)
        chosen = named & (seen == slot)
        seen = seen + named.astype(jnp.int32)
        for p in range(PARTS - 1):
            gather[p * count + t : p * count + t + 1, :] = (chosen & (part == p)).astype(F32)
        for k in range(TOPK):
            row = (PARTS - 1 + k) * count + t
            gather[row : row + 1, :] = (chosen & same[k] & (part == PARTS - 1)).astype(F32)
    sums = gather[...].astype(BF16)
    route = jnp.zeros((TOPK * count, 1), F32)
    for j in range(n_dp):
        block = dot(sums, back_ref[j * lines : (j + 1) * lines, :], ((1,), (0,)))
        for p in range(PARTS - 1):
            width = min(back_wide, rows - p * back_wide)
            if width > 0:
                first = j * rows + p * back_wide
                tokens_ref[:, first : first + width] = block[p * count : (p + 1) * count, :width].astype(BF16)
        if j < CORES:
            terms = block[(PARTS - 1) * count : (PARTS - 1 + TOPK) * count]
            route = route + terms[:, 0:1] + terms[:, 1:2]
    for k in range(TOPK):
        route_ref[:, k : k + 1] = route[k * count : (k + 1) * count]


def call(kernel, outs, *args, scratch=(), flops=0, moved=0, far=(), limit=VMEM_LIMIT):
    args = [pltpu.with_memory_space_constraint(a, pltpu.HBM) if i in far else a for i, a in enumerate(args)]
    return pl.pallas_call(
        kernel,
        out_shape=outs,
        in_specs=[pl.BlockSpec(memory_space=pltpu.HBM if i in far else pltpu.VMEM) for i in range(len(args))],
        out_specs=jax.tree.map(lambda _: pl.BlockSpec(memory_space=pltpu.VMEM), outs),
        scratch_shapes=list(scratch),
        compiler_params=pltpu.CompilerParams(vmem_limit_bytes=limit),
        cost_estimate=pl.CostEstimate(flops=flops, bytes_accessed=moved, transcendentals=0),
    )(*args)


def shape(dims, dtype):
    return jax.ShapeDtypeStruct(dims, dtype)


def local(tokens, cotangent, expert_ids, route_weights, gate_weight, up_weight, down_weight):
    n_dp = lax.axis_size("dp")
    members = lax.axis_size("expert")
    per_expert = members // EXPERTS_F
    sources = n_dp * members
    token_count, model_width = tokens.shape
    rows, hidden_units = gate_weight.shape
    half = hidden_units // CORES
    slots = token_count * TOPK // EXPERTS_F
    count = sources * slots
    per_block = PARTS * slots
    wide = round_up(rows // 2 + 1, LANES)
    back_wide = round_up(-(-rows // (PARTS - 1)), LANES)
    group = math.gcd(sources, 32)

    packed = call(
        functools.partial(pack_kernel, n_dp=n_dp, rows=rows, wide=wide, slots=slots),
        shape((n_dp * EXPERTS_F * per_block, wide), BF16),
        expert_ids,
        route_weights,
        tokens,
        cotangent,
        scratch=[
            pltpu.VMEM(expert_ids.shape, jnp.int32),
            pltpu.VMEM(route_weights.shape, BF16),
            pltpu.VMEM(tokens.shape, BF16),
            pltpu.VMEM(cotangent.shape, BF16),
            pltpu.VMEM((PARTS * token_count, wide), F32),
            pltpu.SemaphoreType.DMA((4,)),
        ],
        moved=1 << 18,
        far=(0, 1, 2, 3),
    )
    packed = packed.reshape(n_dp, EXPERTS_F, per_block, wide)
    if per_expert > 1:
        packed = jnp.repeat(packed, per_expert, axis=1)
    packed = packed.reshape(sources, per_block, wide)
    got = lax.all_to_all(packed, ("dp", "expert"), split_axis=0, concat_axis=0, tiled=True)

    chunks = chunks_of(half)
    width = half // chunks
    cut = half % LANES == 0
    held = pltpu.VMEM((rows, half if cut else hidden_units), BF16)
    held_chunk = pltpu.VMEM((rows, width if cut else hidden_units), BF16)
    gate_other, up_other, down_other = call(
        functools.partial(stage_kernel, half=half),
        [held] * 3,
        packed,
        gate_weight,
        up_weight,
        down_weight,
        scratch=[pltpu.SemaphoreType.DMA((3,))],
        moved=6 * rows * half,
        far=(0, 1, 2, 3),
        limit=1 << 20,
    )

    inputs, upstream, factor, *sends = call(
        functools.partial(send_kernel, rows=rows, wide=wide, slots=slots, half=half),
        [shape((count, rows), BF16), shape((count, rows), BF16), shape((count, 1), F32)]
        + [shape((count, 3 * width), BF16)] * chunks,
        got.reshape(sources * per_block, wide),
        gate_other,
        up_other,
        down_other,
        flops=6 * count * rows * half,
        moved=1 << 20,
    )
    swap = [(i, i ^ 1) for i in range(n_dp)]
    arrived = [lax.ppermute(send, "dp", swap) for send in sends]
    keeps, pairs, gate_owns, up_owns, others = [], [], [], [], []
    for q in range(chunks):
        keep, gate_own, up_own = call(
            functools.partial(keep_kernel, half=half, width=width, q=q),
            [shape((count, 3 * width), F32), held_chunk, held_chunk],
            inputs,
            upstream,
            gate_weight,
            up_weight,
            down_weight,
            scratch=[held_chunk, pltpu.SemaphoreType.DMA((3,))],
            flops=6 * count * rows * width,
            moved=6 * rows * width,
            far=(2, 3, 4),
        )
        pair, low = call(
            pair_kernel,
            [shape((count, 3 * width), F32), shape((count, 3 * width), BF16)],
            keep,
            arrived[q],
            moved=1 << 20,
        )
        gate_owns.append(gate_own)
        up_owns.append(up_own)
        pairs.append(pair)
        passed = []
        for shift in range(1, n_dp // CORES):
            perm = [(i, (i + shift * CORES) % n_dp) for i in range(n_dp)]
            passed.append(lax.ppermute(low, "dp", perm))
        others.append(passed)
    derived, dots, earlier = [], [], []
    for q in range(chunks):
        outs = [shape((count, 3 * width), BF16), shape((count, 1), F32)]
        if q < chunks - 1:
            own, dot_terms, part = call(
                functools.partial(derive_back_kernel, half=width),
                [*outs, shape((count, rows), F32)],
                pairs[q],
                factor,
                gate_owns[q],
                up_owns[q],
                *others[q],
                flops=4 * count * rows * width,
                moved=1 << 20,
            )
            other = lax.ppermute(own, "dp", swap)
            earlier += [part, other]
        else:
            own, dot_terms = call(
                functools.partial(derive_kernel, half=width), outs, pairs[q], factor, *others[q], moved=1 << 20
            )
            other = lax.ppermute(own, "dp", swap)
        derived += [own, other]
        dots.append(dot_terms)
    part = call(
        functools.partial(back_part_kernel, half=half, width=width),
        shape((count, rows), F32),
        own,
        gate_owns[-1],
        up_owns[-1],
        *((gate_other, up_other, *earlier) if earlier else ()),
        flops=4 * count * rows * half,
        moved=1 << 20,
    )
    back = call(
        functools.partial(
            back_kernel,
            half=half,
            width=width,
            first=half - width,
            rows=rows,
            back_wide=back_wide,
            slots=slots,
        ),
        shape((sources * per_block, back_wide), BF16),
        other,
        part,
        gate_other,
        up_other,
        *dots,
        scratch=[
            pltpu.VMEM((count, (PARTS - 1) * back_wide), BF16),
            pltpu.VMEM((group * per_block, back_wide), BF16),
        ],
        flops=4 * count * rows * width,
        moved=1 << 20,
    )
    back = lax.all_to_all(
        back.reshape(sources, per_block, back_wide), ("dp", "expert"), split_axis=0, concat_axis=0, tiled=True
    )
    grads = call(
        functools.partial(grad_kernel, half=half, width=width),
        [shape((rows, hidden_units), BF16)] * 3,
        inputs,
        upstream,
        factor,
        *derived,
        flops=12 * count * rows * half,
        moved=6 * rows * hidden_units,
    )
    d_tokens, d_route = call(
        functools.partial(
            combine_kernel, n_dp=n_dp, rows=rows, back_wide=back_wide, slots=slots, per_expert=per_expert
        ),
        [shape((token_count, model_width), BF16), shape((token_count, TOPK), F32)],
        expert_ids,
        back.reshape(sources * per_block, back_wide),
        scratch=[pltpu.VMEM(((PARTS - 1 + TOPK) * token_count, members * per_block), F32)],
        moved=1 << 18,
    )
    return (d_tokens, d_route, *grads)


def solution(mesh):
    in_specs = (
        P(("dp", "expert"), None),
        P(("dp", "expert"), None),
        P(("dp", "expert"), None),
        P(("dp", "expert"), None),
        P("dp", "expert"),
        P("dp", "expert"),
        P("dp", "expert"),
    )
    out_specs = (
        P(("dp", "expert"), None),
        P(("dp", "expert"), None),
        P("dp", "expert"),
        P("dp", "expert"),
        P("dp", "expert"),
    )
    return jax.shard_map(local, mesh=mesh, in_specs=in_specs, out_specs=out_specs, check_vma=False)
```

```python
import functools
import math

import jax
import jax.numpy as jnp
from jax import lax
from jax.experimental import pallas as pl
from jax.experimental.pallas import tpu as pltpu
from jax.sharding import PartitionSpec as P

EXPERTS_F = 8
TOPK = 4
CORES = 2
LANES = 128
PARTS = 4
BACK_PARTS = 2

SLOPE = 1.702
BF16 = jnp.bfloat16
F32 = jnp.float32
VMEM_LIMIT = 16 * 1024 * 1024


def round_up(value, unit):
    return (value + unit - 1) // unit * unit


def dot(left, right, contract):
    return lax.dot_general(left, right, (contract, ((), ())), preferred_element_type=F32)


def at_half(which, half, width, body):
    if width == half:
        body(0)
    elif half % LANES == 0:
        body(pl.multiple_of(which * half, LANES))
    else:
        for k in range(CORES):
            pl.when(which == k)(functools.partial(body, k * half))


def chunks_of(half):
    return 2 if half % (2 * LANES) == 0 else 1


def window(ref, which, half, first, width):
    if half % LANES:
        return ref
    return ref.at[:, pl.ds(pl.multiple_of(which * half + first, LANES), width)]


def my_core():
    return lax.rem(lax.axis_index("dp"), CORES)


def pack_kernel(*refs, n_dp, rows, wide, slots):
    far, out_ref, near, source, sems = refs[:4], refs[4], refs[5:9], refs[9], refs[10]
    copies = [pltpu.make_async_copy(far[i], near[i], sems.at[i]) for i in range(4)]
    for copy in copies:
        copy.start()
    ids_ref, weights_ref, tokens_ref, grads_ref = near
    count = tokens_ref.shape[0]
    lines = EXPERTS_F * PARTS * slots
    line = lax.broadcasted_iota(jnp.int32, (lines, 1), 0)
    expert = line // (PARTS * slots)
    part = (line // slots) % PARTS
    slot = line % slots
    column = lax.broadcasted_iota(jnp.int32, (lines, PARTS * count), 1)
    source[...] = jnp.zeros_like(source)
    for copy in copies:
        copy.wait()
    ids = ids_ref[...]
    route = weights_ref[...].astype(F32)
    seen = jnp.zeros((lines, 1), jnp.int32)
    factor = jnp.zeros((lines, 1), F32)
    spread = jnp.zeros((lines, PARTS * count), F32)
    for t in range(count):
        named = jnp.zeros((lines, 1), jnp.int32)
        value = jnp.zeros((lines, 1), F32)
        for k in range(TOPK):
            same = ids[t : t + 1, k : k + 1] == expert
            named = named + same.astype(jnp.int32)
            value = value + jnp.where(same, route[t : t + 1, k : k + 1], 0.0)
        chosen = (named > 0) & (seen == slot)
        seen = seen + (named > 0).astype(jnp.int32)
        factor = factor + jnp.where(chosen, value, 0.0)
        spread = spread + jnp.where(chosen & (column == part * count + t), 1.0, 0.0)
    spread = spread.astype(BF16)
    lane = lax.broadcasted_iota(jnp.int32, (lines, wide), 1)
    mark = (lane == rows - wide) & (part % 2 == 1)
    for j in range(n_dp):
        for which, ref in enumerate((tokens_ref, grads_ref)):
            first = 2 * which * count
            source[first : first + count, :] = ref[:, j * rows : j * rows + wide].astype(F32)
            source[first + count : first + 2 * count, 0 : rows - wide] = ref[
                :, j * rows + wide : (j + 1) * rows
            ].astype(F32)
        block = dot(spread, source[...].astype(BF16), ((1,), (0,)))
        out_ref[j * lines : (j + 1) * lines, :] = jnp.where(mark, factor, block).astype(BF16)


def stage_kernel(order_ref, *refs, half):
    fars, nears, sems = refs[:3], refs[3:6], refs[6]
    other = 1 - my_core()
    copies = [
        pltpu.make_async_copy(window(far, other, half, 0, half), near, sems.at[i])
        for i, (far, near) in enumerate(zip(fars, nears))
    ]
    for copy in copies:
        copy.start()
    for copy in copies:
        copy.wait()


def project(base, width, i, left_ref, weight_ref, out_ref):
    product = dot(left_ref[...], weight_ref[:, pl.ds(base, width)], ((1,), (0,)))
    out_ref[:, i * width : (i + 1) * width] = product.astype(out_ref.dtype)


def send_kernel(
    got_ref, gate_ref, up_ref, down_ref, inputs_ref, upstream_ref, factor_ref, send_ref, *, rows, wide, slots, half, width
):
    per_block = PARTS * slots
    sources = got_ref.shape[0] // per_block
    group = math.gcd(sources, 32)
    lines = group * per_block
    lane = lax.broadcasted_iota(jnp.int32, (1, lines), 1)
    target = (lane % per_block) * group + lane // per_block
    move = (lax.broadcasted_iota(jnp.int32, (lines, lines), 0) == target).astype(F32).astype(BF16)
    for g in range(sources // group):
        block = dot(move, got_ref[g * lines : (g + 1) * lines, :], ((1,), (0,)))
        for s in range(slots):
            to = s * sources + g * group
            piece = [block[(p * slots + s) * group : (p * slots + s + 1) * group] for p in range(PARTS)]
            inputs_ref[to : to + group, 0:wide] = piece[0].astype(BF16)
            inputs_ref[to : to + group, wide:rows] = piece[1][:, : rows - wide].astype(BF16)
            upstream_ref[to : to + group, 0:wide] = piece[2].astype(BF16)
            upstream_ref[to : to + group, wide:rows] = piece[3][:, : rows - wide].astype(BF16)
            factor_ref[to : to + group, :] = piece[1][:, rows - wide : rows - wide + 1]

    def body(base):
        for q in range(half // width):
            here = base + q * width
            project(here, width, 3 * q, inputs_ref, gate_ref, send_ref)
            project(here, width, 3 * q + 1, inputs_ref, up_ref, send_ref)
            project(here, width, 3 * q + 2, upstream_ref, down_ref, send_ref)

    at_half(1 - my_core(), half, gate_ref.shape[1], body)


def keep_kernel(inputs_ref, upstream_ref, *refs, half, width, q):
    fars, keep_ref, nears, sems = refs[:3], refs[3], refs[4:7], refs[7]
    core = my_core()
    copies = [
        pltpu.make_async_copy(window(far, core, half, q * width, width), near, sems.at[i])
        for i, (far, near) in enumerate(zip(fars, nears))
    ]
    for copy in copies:
        copy.start()
    for i, (left_ref, near) in enumerate(zip((inputs_ref, inputs_ref, upstream_ref), nears)):
        copies[i].wait()
        at_half(
            core,
            width,
            near.shape[1],
            lambda base, i=i, left_ref=left_ref, near=near: project(base, width, i, left_ref, near, keep_ref),
        )


def pair_kernel(keep_ref, got_ref, pair_ref, low_ref, *, q):
    size = keep_ref.shape[1]
    pair = keep_ref[...] + got_ref[:, q * size : (q + 1) * size].astype(F32)
    pair_ref[...] = pair
    low_ref[...] = pair.astype(BF16)


def derive_kernel(pair_ref, factor_ref, *refs, half):
    others, (own_ref, dots_ref) = refs[:-2], refs[-2:]
    factor = factor_ref[...]

    def total(i):
        columns = slice(i * half, (i + 1) * half)
        value = pair_ref[:, columns]
        for ref in others:
            value = value + ref[:, columns].astype(F32)
        return value

    pre_gate, pre_up, pulled = total(0), total(1), total(2)
    sigma = jax.nn.sigmoid(SLOPE * pre_gate)
    active = pre_gate * sigma
    hidden = (pre_up + 1.0) * active
    d_gate = factor * pulled * (pre_up + 1.0) * sigma * (1.0 + SLOPE * pre_gate * (1.0 - sigma))
    d_up = factor * pulled * active
    own_ref[:, 0:half] = d_gate.astype(BF16)
    own_ref[:, half : 2 * half] = d_up.astype(BF16)
    own_ref[:, 2 * half : 3 * half] = hidden.astype(BF16)
    dots_ref[...] = jnp.sum(hidden * pulled, axis=1, keepdims=True)


def back_product(which, half, width, first, derived_ref, gate_ref, up_ref, write):
    def body(base):
        columns = pl.ds(base + first, width)
        value = dot(derived_ref[:, 0:width], gate_ref[:, columns], ((1,), (1,)))
        value = value + dot(derived_ref[:, width : 2 * width], up_ref[:, columns], ((1,), (1,)))
        write(value)

    at_half(which, half, gate_ref.shape[1], body)


def derive_back_kernel(pair_ref, factor_ref, gate_ref, up_ref, gate_other, up_other, *refs, half):
    others, (own_ref, dots_ref, part_ref, gate_turned, up_turned) = refs[:-5], refs[-5:]
    last = gate_other.shape[1] - half
    gate_turned[...] = gate_other[:, last:].T
    up_turned[...] = up_other[:, last:].T
    derive_kernel(pair_ref, factor_ref, *others, own_ref, dots_ref, half=half)

    def write(value):
        part_ref[...] = value

    back_product(my_core(), half, half, 0, own_ref, gate_ref, up_ref, write)


def back_part_kernel(own_ref, gate_own, up_own, *refs, half, width):
    out_ref = refs[-1]

    def write(value):
        out_ref[...] = value

    def add(value):
        out_ref[...] = out_ref[...] + value

    back_product(my_core(), width, width, 0, own_ref, gate_own, up_own, write)
    if len(refs) > 1:
        gate_other, up_other = refs[:2]
        earlier = refs[2:-1]
        for q in range(len(earlier) // 2):
            out_ref[...] = out_ref[...] + earlier[2 * q][...]
            back_product(1 - my_core(), half, width, q * width, earlier[2 * q + 1], gate_other, up_other, add)


def back_kernel(other_ref, part_ref, gate_ref, up_ref, *refs, half, width, first, rows, back_wide, slots, turned):
    dots_refs, out_ref = refs[:-1], refs[-1]
    per_block = BACK_PARTS * slots
    sources = out_ref.shape[0]
    group = math.gcd(sources, 32)
    lines = group * per_block
    column = lax.broadcasted_iota(jnp.int32, (1, lines), 1)
    target = (column % group) * per_block + column // group
    move = (lax.broadcasted_iota(jnp.int32, (lines, lines), 0) == target).astype(F32).astype(BF16)
    dots = functools.reduce(lambda x, y: x + y, [ref[...] for ref in dots_refs])
    high = dots.astype(BF16).astype(F32)
    tail = rows - back_wide
    lane = lax.broadcasted_iota(jnp.int32, (dots.shape[0], back_wide - tail), 1)
    ending = jnp.where(lane == 0, high, jnp.where(lane == 1, dots - high, 0.0))

    def body(base):
        columns = pl.ds(base + first, width)
        blocks = []
        for lower, upper in ((0, back_wide), (back_wide, rows)):
            value = part_ref[:, lower:upper]
            for i, weight_ref in enumerate((gate_ref, up_ref)):
                left = other_ref[:, i * width : (i + 1) * width]
                if turned:
                    value = value + dot(left, weight_ref[:, lower:upper], ((1,), (0,)))
                else:
                    value = value + dot(left, weight_ref[lower:upper, columns], ((1,), (1,)))
            blocks.append(value)
        blocks[1] = jnp.concatenate([blocks[1], ending], axis=1)
        blocks = [block.astype(BF16) for block in blocks]
        for g in range(sources // group):
            stacked = [
                block[s * sources + g * group : s * sources + (g + 1) * group] for block in blocks for s in range(slots)
            ]
            if sources == group:
                stacked = blocks
            moved = dot(move, jnp.concatenate(stacked, axis=0), ((1,), (0,)))
            out_ref[g * group : (g + 1) * group] = moved.reshape(group, per_block, back_wide).astype(BF16)

    at_half(1 - my_core(), half, half if turned else gate_ref.shape[1], body)


def grad_kernel(inputs_ref, upstream_ref, factor_ref, *refs, half, width):
    derived, outs = refs[:-3], refs[-3:]
    core = my_core()
    scaled = (factor_ref[...] * upstream_ref[...].astype(F32)).astype(BF16)
    lefts = (inputs_ref[...], inputs_ref[...], scaled)
    for n, ref in enumerate(derived):

        def body(base, n=n, ref=ref):
            columns = pl.ds(base + (n // CORES) * width, width)
            for i, (left, out) in enumerate(zip(lefts, outs)):
                product = dot(left, ref[:, i * width : (i + 1) * width], ((0,), (0,)))
                out[:, columns] = product.astype(BF16)

        at_half(core if n % CORES == 0 else 1 - core, half, outs[0].shape[1], body)


def combine_kernel(ids_ref, back_ref, tokens_ref, route_ref, gather, *, n_dp, rows, back_wide, slots, per_expert):
    count = tokens_ref.shape[0]
    per_block = BACK_PARTS * slots
    members = back_ref.shape[0] // n_dp
    lines = members * per_block
    line = lax.broadcasted_iota(jnp.int32, (1, lines), 1)
    expert = line // (per_block * per_expert)
    part = (line // slots) % BACK_PARTS
    slot = line % slots
    ids = ids_ref[...]
    seen = jnp.zeros((1, lines), jnp.int32)
    for t in range(count):
        same = [ids[t : t + 1, k : k + 1] == expert for k in range(TOPK)]
        named = functools.reduce(lambda a, b: a | b, same)
        chosen = named & (seen == slot)
        seen = seen + named.astype(jnp.int32)
        for p in range(BACK_PARTS):
            gather[p * count + t : p * count + t + 1, :] = (chosen & (part == p)).astype(F32)
        for k in range(TOPK):
            row = (BACK_PARTS + k) * count + t
            gather[row : row + 1, :] = (chosen & same[k] & (part == BACK_PARTS - 1)).astype(F32)
    sums = gather[...].astype(BF16)
    route = jnp.zeros((TOPK * count, 1), F32)
    tail = rows - back_wide
    for j in range(n_dp):
        arrived = back_ref[j * members : (j + 1) * members].astype(F32).reshape(lines, back_wide).astype(BF16)
        block = dot(sums, arrived, ((1,), (0,)))
        tokens_ref[:, j * rows : j * rows + back_wide] = block[0:count].astype(BF16)
        tokens_ref[:, j * rows + back_wide : (j + 1) * rows] = block[count : 2 * count, :tail].astype(BF16)
        if j < CORES:
            terms = block[BACK_PARTS * count :]
            route = route + terms[:, tail : tail + 1] + terms[:, tail + 1 : tail + 2]
    for k in range(TOPK):
        route_ref[:, k : k + 1] = route[k * count : (k + 1) * count]


def call(kernel, outs, *args, scratch=(), flops=0, moved=0, far=(), limit=VMEM_LIMIT):
    args = [pltpu.with_memory_space_constraint(a, pltpu.HBM) if i in far else a for i, a in enumerate(args)]
    return pl.pallas_call(
        kernel,
        out_shape=outs,
        in_specs=[pl.BlockSpec(memory_space=pltpu.HBM if i in far else pltpu.VMEM) for i in range(len(args))],
        out_specs=jax.tree.map(lambda _: pl.BlockSpec(memory_space=pltpu.VMEM), outs),
        scratch_shapes=list(scratch),
        compiler_params=pltpu.CompilerParams(vmem_limit_bytes=limit),
        cost_estimate=pl.CostEstimate(flops=flops, bytes_accessed=moved, transcendentals=0),
    )(*args)


def shape(dims, dtype):
    return jax.ShapeDtypeStruct(dims, dtype)


def local(tokens, cotangent, expert_ids, route_weights, gate_weight, up_weight, down_weight):
    n_dp = lax.axis_size("dp")
    members = lax.axis_size("expert")
    per_expert = members // EXPERTS_F
    sources = n_dp * members
    token_count, model_width = tokens.shape
    rows, hidden_units = gate_weight.shape
    half = hidden_units // CORES
    slots = token_count * TOPK // EXPERTS_F
    count = sources * slots
    per_block = PARTS * slots
    wide = round_up(rows // 2 + 1, LANES)
    back_wide = round_up(rows // BACK_PARTS + 1, LANES)

    packed = call(
        functools.partial(pack_kernel, n_dp=n_dp, rows=rows, wide=wide, slots=slots),
        shape((n_dp * EXPERTS_F * per_block, wide), BF16),
        expert_ids,
        route_weights,
        tokens,
        cotangent,
        scratch=[
            pltpu.VMEM(expert_ids.shape, jnp.int32),
            pltpu.VMEM(route_weights.shape, BF16),
            pltpu.VMEM(tokens.shape, BF16),
            pltpu.VMEM(cotangent.shape, BF16),
            pltpu.VMEM((PARTS * token_count, wide), F32),
            pltpu.SemaphoreType.DMA((4,)),
        ],
        moved=1 << 18,
        far=(0, 1, 2, 3),
    )
    packed = packed.reshape(n_dp, EXPERTS_F, per_block, wide)
    if per_expert > 1:
        packed = jnp.repeat(packed, per_expert, axis=1)
    packed = packed.reshape(sources, per_block, wide)
    got = lax.all_to_all(packed, ("dp", "expert"), split_axis=0, concat_axis=0, tiled=True)

    chunks = chunks_of(half)
    width = half // chunks
    cut = half % LANES == 0
    held = pltpu.VMEM((rows, half if cut else hidden_units), BF16)
    held_chunk = pltpu.VMEM((rows, width if cut else hidden_units), BF16)
    gate_other, up_other, down_other = call(
        functools.partial(stage_kernel, half=half),
        [held] * 3,
        packed,
        gate_weight,
        up_weight,
        down_weight,
        scratch=[pltpu.SemaphoreType.DMA((3,))],
        moved=6 * rows * half,
        far=(0, 1, 2, 3),
        limit=1 << 20,
    )

    inputs, upstream, factor, send = call(
        functools.partial(send_kernel, rows=rows, wide=wide, slots=slots, half=half, width=width),
        [shape((count, rows), BF16), shape((count, rows), BF16), shape((count, 1), F32), shape((count, 3 * half), BF16)],
        got.reshape(sources * per_block, wide),
        gate_other,
        up_other,
        down_other,
        flops=6 * count * rows * half,
        moved=1 << 20,
    )
    swap = [(i, i ^ 1) for i in range(n_dp)]
    arrived = lax.ppermute(send, "dp", swap)
    keeps, pairs, gate_owns, up_owns, others = [], [], [], [], []
    for q in range(chunks):
        keep, gate_own, up_own = call(
            functools.partial(keep_kernel, half=half, width=width, q=q),
            [shape((count, 3 * width), F32), held_chunk, held_chunk],
            inputs,
            upstream,
            gate_weight,
            up_weight,
            down_weight,
            scratch=[held_chunk, pltpu.SemaphoreType.DMA((3,))],
            flops=6 * count * rows * width,
            moved=6 * rows * width,
            far=(2, 3, 4),
        )
        pair, low = call(
            functools.partial(pair_kernel, q=q),
            [shape((count, 3 * width), F32), shape((count, 3 * width), BF16)],
            keep,
            arrived,
            moved=1 << 20,
        )
        gate_owns.append(gate_own)
        up_owns.append(up_own)
        pairs.append(pair)
        passed = []
        for shift in range(1, n_dp // CORES):
            perm = [(i, (i + shift * CORES) % n_dp) for i in range(n_dp)]
            passed.append(lax.ppermute(low, "dp", perm))
        others.append(passed)
    derived, dots, earlier, turned = [], [], [], []
    for q in range(chunks):
        outs = [shape((count, 3 * width), BF16), shape((count, 1), F32)]
        if q < chunks - 1:
            own, dot_terms, part, *turned = call(
                functools.partial(derive_back_kernel, half=width),
                [*outs, shape((count, rows), F32), shape((width, rows), BF16), shape((width, rows), BF16)],
                pairs[q],
                factor,
                gate_owns[q],
                up_owns[q],
                gate_other,
                up_other,
                *others[q],
                flops=4 * count * rows * width,
                moved=1 << 20,
            )
            other = lax.ppermute(own, "dp", swap)
            earlier += [part, other]
        else:
            own, dot_terms = call(
                functools.partial(derive_kernel, half=width), outs, pairs[q], factor, *others[q], moved=1 << 20
            )
            other = lax.ppermute(own, "dp", swap)
        derived += [own, other]
        dots.append(dot_terms)
    part = call(
        functools.partial(back_part_kernel, half=half, width=width),
        shape((count, rows), F32),
        own,
        gate_owns[-1],
        up_owns[-1],
        *((gate_other, up_other, *earlier) if earlier else ()),
        flops=4 * count * rows * half,
        moved=1 << 20,
    )
    back = call(
        functools.partial(
            back_kernel,
            half=half,
            width=width,
            first=half - width,
            rows=rows,
            back_wide=back_wide,
            slots=slots,
            turned=bool(turned),
        ),
        shape((sources, BACK_PARTS * slots, back_wide), BF16),
        other,
        part,
        *(turned or (gate_other, up_other)),
        *dots,
        flops=4 * count * rows * width,
        moved=1 << 20,
    )
    back = lax.all_to_all(back, ("dp", "expert"), split_axis=0, concat_axis=0, tiled=True)
    grads = call(
        functools.partial(grad_kernel, half=half, width=width),
        [shape((rows, hidden_units), BF16)] * 3,
        inputs,
        upstream,
        factor,
        *derived,
        flops=12 * count * rows * half,
        moved=6 * rows * hidden_units,
    )
    d_tokens, d_route = call(
        functools.partial(
            combine_kernel, n_dp=n_dp, rows=rows, back_wide=back_wide, slots=slots, per_expert=per_expert
        ),
        [shape((token_count, model_width), BF16), shape((token_count, TOPK), F32)],
        expert_ids,
        back,
        scratch=[pltpu.VMEM(((BACK_PARTS + TOPK) * token_count, members * BACK_PARTS * slots), F32)],
        moved=1 << 18,
    )
    return (d_tokens, d_route, *grads)


def solution(mesh):
    in_specs = (
        P(("dp", "expert"), None),
        P(("dp", "expert"), None),
        P(("dp", "expert"), None),
        P(("dp", "expert"), None),
        P("dp", "expert"),
        P("dp", "expert"),
        P("dp", "expert"),
    )
    out_specs = (
        P(("dp", "expert"), None),
        P(("dp", "expert"), None),
        P("dp", "expert"),
        P("dp", "expert"),
        P("dp", "expert"),
    )
    return jax.shard_map(local, mesh=mesh, in_specs=in_specs, out_specs=out_specs, check_vma=False)
```

```python
import functools
import math

import jax
import jax.numpy as jnp
from jax import lax
from jax.experimental import pallas as pl
from jax.experimental.pallas import tpu as pltpu
from jax.sharding import PartitionSpec as P

EXPERTS_F = 8
TOPK = 4
CORES = 2
LANES = 128
PARTS = 4
BACK_PARTS = 2

SLOPE = 1.702
BF16 = jnp.bfloat16
F32 = jnp.float32
VMEM_LIMIT = 16 * 1024 * 1024


def round_up(value, unit):
    return (value + unit - 1) // unit * unit


def dot(left, right, contract):
    return lax.dot_general(left, right, (contract, ((), ())), preferred_element_type=F32)


def at_half(which, half, width, body):
    if width == half:
        body(0)
    elif half % LANES == 0:
        body(pl.multiple_of(which * half, LANES))
    else:
        for k in range(CORES):
            pl.when(which == k)(functools.partial(body, k * half))


def chunks_of(half):
    return 2 if half % (2 * LANES) == 0 else 1


def window(ref, which, half, first, width):
    if half % LANES:
        return ref
    return ref.at[:, pl.ds(pl.multiple_of(which * half + first, LANES), width)]


def my_core():
    return lax.rem(lax.axis_index("dp"), CORES)


def pack_kernel(*refs, n_dp, rows, wide, slots):
    far, out_ref, near, (source, spread, sems) = refs[:4], refs[4], refs[5:9], refs[9:]
    copies = [pltpu.make_async_copy(far[i], near[i], sems.at[i]) for i in range(4)]
    for copy in copies:
        copy.start()
    ids_ref, weights_ref, tokens_ref, grads_ref = near
    count = tokens_ref.shape[0]
    taken = PARTS * count
    lines = EXPERTS_F * PARTS * slots
    line = lax.broadcasted_iota(jnp.int32, (1, lines), 1)
    expert = line // (PARTS * slots)
    part = (line // slots) % PARTS
    slot = line % slots
    single = lax.broadcasted_iota(jnp.int32, source.shape[1:], 0) == taken
    single = single & (lax.broadcasted_iota(jnp.int32, source.shape[1:], 1) == rows - wide)
    for j in range(n_dp):
        source[j] = single.astype(F32)
    spread[...] = jnp.zeros_like(spread)
    for copy in copies:
        copy.wait()
    ids = ids_ref[...]
    route = weights_ref[...].astype(F32)
    seen = jnp.zeros((1, lines), jnp.int32)
    factor = jnp.zeros((1, lines), F32)
    for t in range(count):
        same = [ids[t : t + 1, k : k + 1] == expert for k in range(TOPK)]
        named = functools.reduce(lambda a, b: a | b, same)
        chosen = named & (seen == slot)
        seen = seen + named.astype(jnp.int32)
        for k in range(TOPK):
            factor = factor + jnp.where(chosen & same[k], route[t : t + 1, k : k + 1], 0.0)
        for p in range(PARTS):
            spread[p * count + t : p * count + t + 1, :] = (chosen & (part == p)).astype(F32)
    spread[taken : taken + 1, :] = jnp.where(part % 2 == 1, factor, 0.0)
    move = spread[...].astype(BF16)
    for j in range(n_dp):
        for which, ref in enumerate((tokens_ref, grads_ref)):
            first = 2 * which * count
            source[j, first : first + count, :] = ref[:, j * rows : j * rows + wide].astype(F32)
            source[j, first + count : first + 2 * count, 0 : rows - wide] = ref[
                :, j * rows + wide : (j + 1) * rows
            ].astype(F32)
    for j in range(n_dp):
        block = dot(move, source[j].astype(BF16), ((0,), (0,)))
        out_ref[j * lines : (j + 1) * lines, :] = block.astype(BF16)


def stage_kernel(order_ref, *refs, half):
    fars, nears, sems = refs[:3], refs[3:6], refs[6]
    other = 1 - my_core()
    copies = [
        pltpu.make_async_copy(window(far, other, half, 0, half), near, sems.at[i])
        for i, (far, near) in enumerate(zip(fars, nears))
    ]
    for copy in copies:
        copy.start()
    for copy in copies:
        copy.wait()


def project(base, width, i, left_ref, weight_ref, out_ref):
    product = dot(left_ref[...], weight_ref[:, pl.ds(base, width)], ((1,), (0,)))
    out_ref[:, i * width : (i + 1) * width] = product.astype(out_ref.dtype)


def send_kernel(
    got_ref, gate_ref, up_ref, down_ref, inputs_ref, upstream_ref, factor_ref, send_ref, *, rows, wide, slots, half, width
):
    per_block = PARTS * slots
    sources = got_ref.shape[0] // per_block
    group = math.gcd(sources, 32)
    lines = group * per_block
    lane = lax.broadcasted_iota(jnp.int32, (1, lines), 1)
    target = (lane % per_block) * group + lane // per_block
    move = (lax.broadcasted_iota(jnp.int32, (lines, lines), 0) == target).astype(F32).astype(BF16)
    for g in range(sources // group):
        block = dot(move, got_ref[g * lines : (g + 1) * lines, :], ((1,), (0,)))
        for s in range(slots):
            to = s * sources + g * group
            piece = [block[(p * slots + s) * group : (p * slots + s + 1) * group] for p in range(PARTS)]
            inputs_ref[to : to + group, 0:wide] = piece[0].astype(BF16)
            inputs_ref[to : to + group, wide:rows] = piece[1][:, : rows - wide].astype(BF16)
            upstream_ref[to : to + group, 0:wide] = piece[2].astype(BF16)
            upstream_ref[to : to + group, wide:rows] = piece[3][:, : rows - wide].astype(BF16)
            factor_ref[to : to + group, :] = piece[1][:, rows - wide : rows - wide + 1]

    def body(base):
        for q in range(half // width):
            here = base + q * width
            project(here, width, 3 * q, inputs_ref, gate_ref, send_ref)
            project(here, width, 3 * q + 1, inputs_ref, up_ref, send_ref)
            project(here, width, 3 * q + 2, upstream_ref, down_ref, send_ref)

    at_half(1 - my_core(), half, gate_ref.shape[1], body)


def keep_kernel(inputs_ref, upstream_ref, *refs, half, width, q):
    fars, keep_ref, nears, sems = refs[:3], refs[3], refs[4:7], refs[7]
    core = my_core()
    copies = [
        pltpu.make_async_copy(window(far, core, half, q * width, width), near, sems.at[i])
        for i, (far, near) in enumerate(zip(fars, nears))
    ]
    for copy in copies:
        copy.start()
    for i, (left_ref, near) in enumerate(zip((inputs_ref, inputs_ref, upstream_ref), nears)):
        copies[i].wait()
        at_half(
            core,
            width,
            near.shape[1],
            lambda base, i=i, left_ref=left_ref, near=near: project(base, width, i, left_ref, near, keep_ref),
        )


def pair_kernel(keep_ref, got_ref, pair_ref, low_ref, *, q):
    size = keep_ref.shape[1]
    pair = keep_ref[...] + got_ref[:, q * size : (q + 1) * size].astype(F32)
    pair_ref[...] = pair
    low_ref[...] = pair.astype(BF16)


def derive_kernel(pair_ref, factor_ref, *refs, half):
    others, (own_ref, dots_ref) = refs[:-2], refs[-2:]
    factor = factor_ref[...]

    def total(i):
        columns = slice(i * half, (i + 1) * half)
        value = pair_ref[:, columns]
        for ref in others:
            value = value + ref[:, columns].astype(F32)
        return value

    pre_gate, pre_up, pulled = total(0), total(1), total(2)
    sigma = jax.nn.sigmoid(SLOPE * pre_gate)
    active = pre_gate * sigma
    hidden = (pre_up + 1.0) * active
    d_gate = factor * pulled * (pre_up + 1.0) * sigma * (1.0 + SLOPE * pre_gate * (1.0 - sigma))
    d_up = factor * pulled * active
    own_ref[:, 0:half] = d_gate.astype(BF16)
    own_ref[:, half : 2 * half] = d_up.astype(BF16)
    own_ref[:, 2 * half : 3 * half] = hidden.astype(BF16)
    dots_ref[...] = jnp.sum(hidden * pulled, axis=1, keepdims=True)


def back_product(which, half, width, first, derived_ref, gate_ref, up_ref, write):
    def body(base):
        columns = pl.ds(base + first, width)
        value = dot(derived_ref[:, 0:width], gate_ref[:, columns], ((1,), (1,)))
        value = value + dot(derived_ref[:, width : 2 * width], up_ref[:, columns], ((1,), (1,)))
        write(value)

    at_half(which, half, gate_ref.shape[1], body)


def derive_back_kernel(pair_ref, factor_ref, gate_ref, up_ref, gate_other, up_other, *refs, half):
    others, (own_ref, dots_ref, part_ref, gate_turned, up_turned) = refs[:-5], refs[-5:]
    last = gate_other.shape[1] - half
    gate_turned[...] = gate_other[:, last:].T
    up_turned[...] = up_other[:, last:].T
    derive_kernel(pair_ref, factor_ref, *others, own_ref, dots_ref, half=half)

    def write(value):
        part_ref[...] = value

    back_product(my_core(), half, half, 0, own_ref, gate_ref, up_ref, write)


def back_part_kernel(own_ref, gate_own, up_own, *refs, half, width, chunks, tail, slots):
    dots_refs, (out_ref, move_ref, ending_ref) = refs[:chunks], refs[-3:]
    refs = (*refs[chunks:-3], out_ref)
    per_block = BACK_PARTS * slots
    lines = move_ref.shape[0]
    group = lines // per_block
    column = lax.broadcasted_iota(jnp.int32, (1, lines), 1)
    target = (column % group) * per_block + column // group
    move_ref[...] = (lax.broadcasted_iota(jnp.int32, (lines, lines), 0) == target).astype(F32).astype(BF16)
    dots = functools.reduce(lambda x, y: x + y, [ref[...] for ref in dots_refs])
    high = dots.astype(BF16).astype(F32)
    lane = lax.broadcasted_iota(jnp.int32, ending_ref.shape, 1)
    ending = jnp.where(lane == tail, high, jnp.where(lane == tail + 1, dots - high, 0.0))
    ending_ref[...] = ending.astype(BF16)

    def write(value):
        out_ref[...] = value

    def add(value):
        out_ref[...] = out_ref[...] + value

    back_product(my_core(), width, width, 0, own_ref, gate_own, up_own, write)
    if len(refs) > 1:
        gate_other, up_other = refs[:2]
        earlier = refs[2:-1]
        for q in range(len(earlier) // 2):
            out_ref[...] = out_ref[...] + earlier[2 * q][...]
            back_product(1 - my_core(), half, width, q * width, earlier[2 * q + 1], gate_other, up_other, add)


def back_kernel(
    other_ref, part_ref, move_ref, ending_ref, gate_ref, up_ref, out_ref, *, half, width, first, rows, slots, turned
):
    sources, per_block, back_wide = out_ref.shape
    group = move_ref.shape[0] // per_block

    def body(base):
        columns = pl.ds(base + first, width)
        blocks = []
        for lower, upper in ((0, back_wide), (back_wide, rows)):
            value = part_ref[:, lower:upper]
            for i, weight_ref in enumerate((gate_ref, up_ref)):
                left = other_ref[:, i * width : (i + 1) * width]
                if turned:
                    value = value + dot(left, weight_ref[:, lower:upper], ((1,), (0,)))
                else:
                    value = value + dot(left, weight_ref[lower:upper, columns], ((1,), (1,)))
            blocks.append(value)
        blocks = [block.astype(BF16) for block in blocks]
        blocks[1] = jnp.concatenate([blocks[1], ending_ref[:, rows - back_wide :]], axis=1)
        for g in range(sources // group):
            stacked = [
                block[s * sources + g * group : s * sources + (g + 1) * group] for block in blocks for s in range(slots)
            ]
            if sources == group:
                stacked = blocks
            moved = dot(move_ref[...], jnp.concatenate(stacked, axis=0), ((1,), (0,)))
            out_ref[g * group : (g + 1) * group] = moved.reshape(group, per_block, back_wide).astype(BF16)

    at_half(1 - my_core(), half, half if turned else gate_ref.shape[1], body)


def grad_kernel(ids_ref, inputs_ref, upstream_ref, factor_ref, *refs, half, width, slots, per_expert):
    derived, outs, (sums_ref, gather) = refs[:-5], refs[-5:-2], refs[-2:]
    select_rows(ids_ref, gather, sums_ref, slots, per_expert)
    core = my_core()
    scaled = (factor_ref[...] * upstream_ref[...].astype(F32)).astype(BF16)
    lefts = (inputs_ref[...], inputs_ref[...], scaled)
    for n, ref in enumerate(derived):

        def body(base, n=n, ref=ref):
            columns = pl.ds(base + (n // CORES) * width, width)
            for i, (left, out) in enumerate(zip(lefts, outs)):
                product = dot(left, ref[:, i * width : (i + 1) * width], ((0,), (0,)))
                out[:, columns] = product.astype(BF16)

        at_half(core if n % CORES == 0 else 1 - core, half, outs[0].shape[1], body)


def select_rows(ids_ref, gather, sums_ref, slots, per_expert):
    count = ids_ref.shape[0]
    lines = gather.shape[1]
    line = lax.broadcasted_iota(jnp.int32, (1, lines), 1)
    expert = line // (BACK_PARTS * slots * per_expert)
    part = (line // slots) % BACK_PARTS
    slot = line % slots
    ids = ids_ref[...]
    seen = jnp.zeros((1, lines), jnp.int32)
    for t in range(count):
        same = [ids[t : t + 1, k : k + 1] == expert for k in range(TOPK)]
        named = functools.reduce(lambda a, b: a | b, same)
        chosen = named & (seen == slot)
        seen = seen + named.astype(jnp.int32)
        for p in range(BACK_PARTS):
            gather[p * count + t : p * count + t + 1, :] = (chosen & (part == p)).astype(F32)
        for k in range(TOPK):
            row = (BACK_PARTS + k) * count + t
            gather[row : row + 1, :] = (chosen & same[k] & (part == BACK_PARTS - 1)).astype(F32)
    sums_ref[...] = gather[...].astype(BF16)


def combine_kernel(sums_ref, back_ref, tokens_ref, route_ref, *, n_dp, rows, back_wide):
    count = tokens_ref.shape[0]
    members = back_ref.shape[0] // n_dp
    lines = sums_ref.shape[1]
    sums = sums_ref[...]
    route = jnp.zeros((TOPK * count, 1), F32)
    tail = rows - back_wide
    for j in range(n_dp):
        arrived = back_ref[j * members : (j + 1) * members].astype(F32).reshape(lines, back_wide).astype(BF16)
        block = dot(sums, arrived, ((1,), (0,)))
        tokens_ref[:, j * rows : j * rows + back_wide] = block[0:count].astype(BF16)
        tokens_ref[:, j * rows + back_wide : (j + 1) * rows] = block[count : 2 * count, :tail].astype(BF16)
        if j < CORES:
            terms = block[BACK_PARTS * count :]
            route = route + terms[:, tail : tail + 1] + terms[:, tail + 1 : tail + 2]
    for k in range(TOPK):
        route_ref[:, k : k + 1] = route[k * count : (k + 1) * count]


def call(kernel, outs, *args, scratch=(), flops=0, moved=0, far=(), limit=VMEM_LIMIT):
    args = [pltpu.with_memory_space_constraint(a, pltpu.HBM) if i in far else a for i, a in enumerate(args)]
    return pl.pallas_call(
        kernel,
        out_shape=outs,
        in_specs=[pl.BlockSpec(memory_space=pltpu.HBM if i in far else pltpu.VMEM) for i in range(len(args))],
        out_specs=jax.tree.map(lambda _: pl.BlockSpec(memory_space=pltpu.VMEM), outs),
        scratch_shapes=list(scratch),
        compiler_params=pltpu.CompilerParams(vmem_limit_bytes=limit),
        cost_estimate=pl.CostEstimate(flops=flops, bytes_accessed=moved, transcendentals=0),
    )(*args)


def shape(dims, dtype):
    return jax.ShapeDtypeStruct(dims, dtype)


def local(tokens, cotangent, expert_ids, route_weights, gate_weight, up_weight, down_weight):
    n_dp = lax.axis_size("dp")
    members = lax.axis_size("expert")
    per_expert = members // EXPERTS_F
    sources = n_dp * members
    token_count, model_width = tokens.shape
    rows, hidden_units = gate_weight.shape
    half = hidden_units // CORES
    slots = token_count * TOPK // EXPERTS_F
    count = sources * slots
    per_block = PARTS * slots
    wide = round_up(rows // 2 + 1, LANES)
    back_wide = round_up(rows // BACK_PARTS + 1, LANES)

    packed = call(
        functools.partial(pack_kernel, n_dp=n_dp, rows=rows, wide=wide, slots=slots),
        shape((n_dp * EXPERTS_F * per_block, wide), BF16),
        expert_ids,
        route_weights,
        tokens,
        cotangent,
        scratch=[
            pltpu.VMEM(expert_ids.shape, jnp.int32),
            pltpu.VMEM(route_weights.shape, BF16),
            pltpu.VMEM(tokens.shape, BF16),
            pltpu.VMEM(cotangent.shape, BF16),
            pltpu.VMEM((n_dp, round_up(PARTS * token_count + 1, 8), wide), F32),
            pltpu.VMEM((round_up(PARTS * token_count + 1, 8), EXPERTS_F * per_block), F32),
            pltpu.SemaphoreType.DMA((4,)),
        ],
        moved=1 << 18,
        far=(0, 1, 2, 3),
    )
    packed = packed.reshape(n_dp, EXPERTS_F, per_block, wide)
    if per_expert > 1:
        packed = jnp.repeat(packed, per_expert, axis=1)
    packed = packed.reshape(sources, per_block, wide)
    got = lax.all_to_all(packed, ("dp", "expert"), split_axis=0, concat_axis=0, tiled=True)

    chunks = chunks_of(half)
    width = half // chunks
    cut = half % LANES == 0
    held = pltpu.VMEM((rows, half if cut else hidden_units), BF16)
    held_chunk = pltpu.VMEM((rows, width if cut else hidden_units), BF16)
    gate_other, up_other, down_other = call(
        functools.partial(stage_kernel, half=half),
        [held] * 3,
        packed,
        gate_weight,
        up_weight,
        down_weight,
        scratch=[pltpu.SemaphoreType.DMA((3,))],
        moved=6 * rows * half,
        far=(0, 1, 2, 3),
        limit=1 << 20,
    )

    inputs, upstream, factor, send = call(
        functools.partial(send_kernel, rows=rows, wide=wide, slots=slots, half=half, width=width),
        [shape((count, rows), BF16), shape((count, rows), BF16), shape((count, 1), F32), shape((count, 3 * half), BF16)],
        got.reshape(sources * per_block, wide),
        gate_other,
        up_other,
        down_other,
        flops=6 * count * rows * half,
        moved=1 << 20,
    )
    swap = [(i, i ^ 1) for i in range(n_dp)]
    arrived = lax.ppermute(send, "dp", swap)
    keeps, pairs, gate_owns, up_owns, others = [], [], [], [], []
    for q in range(chunks):
        keep, gate_own, up_own = call(
            functools.partial(keep_kernel, half=half, width=width, q=q),
            [shape((count, 3 * width), F32), held_chunk, held_chunk],
            inputs,
            upstream,
            gate_weight,
            up_weight,
            down_weight,
            scratch=[held_chunk, pltpu.SemaphoreType.DMA((3,))],
            flops=6 * count * rows * width,
            moved=6 * rows * width,
            far=(2, 3, 4),
        )
        pair, low = call(
            functools.partial(pair_kernel, q=q),
            [shape((count, 3 * width), F32), shape((count, 3 * width), BF16)],
            keep,
            arrived,
            moved=1 << 20,
        )
        gate_owns.append(gate_own)
        up_owns.append(up_own)
        pairs.append(pair)
        passed = []
        for shift in range(1, n_dp // CORES):
            perm = [(i, (i + shift * CORES) % n_dp) for i in range(n_dp)]
            passed.append(lax.ppermute(low, "dp", perm))
        others.append(passed)
    derived, dots, earlier, turned = [], [], [], []
    for q in range(chunks):
        outs = [shape((count, 3 * width), BF16), shape((count, 1), F32)]
        if q < chunks - 1:
            own, dot_terms, part, *turned = call(
                functools.partial(derive_back_kernel, half=width),
                [*outs, shape((count, rows), F32), shape((width, rows), BF16), shape((width, rows), BF16)],
                pairs[q],
                factor,
                gate_owns[q],
                up_owns[q],
                gate_other,
                up_other,
                *others[q],
                flops=4 * count * rows * width,
                moved=1 << 20,
            )
            other = lax.ppermute(own, "dp", swap)
            earlier += [part, other]
        else:
            own, dot_terms = call(
                functools.partial(derive_kernel, half=width), outs, pairs[q], factor, *others[q], moved=1 << 20
            )
            other = lax.ppermute(own, "dp", swap)
        derived += [own, other]
        dots.append(dot_terms)
    lines = math.gcd(sources, 32) * BACK_PARTS * slots
    part, move, ending = call(
        functools.partial(
            back_part_kernel, half=half, width=width, chunks=chunks, tail=rows - back_wide, slots=slots
        ),
        [shape((count, rows), F32), shape((lines, lines), BF16), shape((count, back_wide), BF16)],
        own,
        gate_owns[-1],
        up_owns[-1],
        *dots,
        *((gate_other, up_other, *earlier) if earlier else ()),
        flops=4 * count * rows * half,
        moved=1 << 20,
    )
    back = call(
        functools.partial(
            back_kernel,
            half=half,
            width=width,
            first=half - width,
            rows=rows,
            slots=slots,
            turned=bool(turned),
        ),
        shape((sources, BACK_PARTS * slots, back_wide), BF16),
        other,
        part,
        move,
        ending,
        *(turned or (gate_other, up_other)),
        flops=4 * count * rows * width,
        moved=1 << 20,
    )
    back = lax.all_to_all(back, ("dp", "expert"), split_axis=0, concat_axis=0, tiled=True)
    select = ((BACK_PARTS + TOPK) * token_count, members * BACK_PARTS * slots)
    *grads, sums = call(
        functools.partial(grad_kernel, half=half, width=width, slots=slots, per_expert=per_expert),
        [shape((rows, hidden_units), BF16)] * 3 + [shape(select, BF16)],
        expert_ids,
        inputs,
        upstream,
        factor,
        *derived,
        scratch=[pltpu.VMEM(select, F32)],
        flops=12 * count * rows * half,
        moved=6 * rows * hidden_units,
    )
    d_tokens, d_route = call(
        functools.partial(combine_kernel, n_dp=n_dp, rows=rows, back_wide=back_wide),
        [shape((token_count, model_width), BF16), shape((token_count, TOPK), F32)],
        sums,
        back,
        moved=1 << 18,
    )
    return (d_tokens, d_route, *grads)


def solution(mesh):
    in_specs = (
        P(("dp", "expert"), None),
        P(("dp", "expert"), None),
        P(("dp", "expert"), None),
        P(("dp", "expert"), None),
        P("dp", "expert"),
        P("dp", "expert"),
        P("dp", "expert"),
    )
    out_specs = (
        P(("dp", "expert"), None),
        P(("dp", "expert"), None),
        P("dp", "expert"),
        P("dp", "expert"),
        P("dp", "expert"),
    )
    return jax.shard_map(local, mesh=mesh, in_specs=in_specs, out_specs=out_specs, check_vma=False)
```
